32 devices in a mesh: rows: 8 (over z, y), heads: 4 (over x, core).
Axes of the slice: x: 2, y: 2, z: 4, core: 2. Of those that a mesh axis runs over, the one named last changes fastest.
Arguments:
- queries: bfloat16 [4096, 512], P('rows', 'heads'), may hold values from -6 to 6
- key_vectors: bfloat16 [4096, 512], P('rows', 'heads'), may hold values from -6 to 6
- value_vectors: bfloat16 [4096, 512], P('rows', 'heads'), may hold values from -120 to 120
- gating: bfloat16 [4096, 512], P('rows', 'heads'), may hold values from -6 to 6
- bounds: int32 [2, 4096], P(None, 'rows'), may hold values from 0 to 4095, as said below
- cotangent: bfloat16 [4096, 512], P('rows', 'heads'), may hold values from -6 to 6
Outputs:
- layer_out: bfloat16 [4096, 512], P('rows', 'heads')
- grad_queries: bfloat16 [4096, 512], P('rows', 'heads')
- grad_keys: bfloat16 [4096, 512], P('rows', 'heads')
- grad_values: bfloat16 [4096, 512], P('rows', 'heads')
- grad_gating: bfloat16 [4096, 512], P('rows', 'heads')
The draws below stay inside these ranges and needn't reach their ends.
Inputs may be any that keep to these rules, and one draw needn't show every extreme that they name: bounds[0, r] and bounds[1, r] are the first and the last row of the history that holds row r; histories are runs of consecutive rows that cover all 4096 rows, each at most 1024 rows long, and one of them exactly that long.
All inputs are finite; a program needn't handle non-finite values.
Results may differ from the reference program's by a relative error of at most 0.006.
Values may be sent and summed in bfloat16 or wider, within the bound.
No kernel may reach another device: no remote copies, remote signals or barrier semaphores. Data moves between devices by JAX's collectives and lax.ppermute only.
A program may use at most 64 MiB of HBM per device.

```python
import math
import jax
import jax.numpy as jnp
from jax import lax

DH = 128
ROWS_DEV = 512
REACH = 2
HEADS = 4
TOTAL = 4096


def draw_bounds(key, part):
    longest = REACH * ROWS_DEV
    cut_row = TOTAL - longest - 1
    first_key, second_key = jax.random.split(jax.random.fold_in(key, 7), 2)
    halvings = jax.random.randint(first_key, (TOTAL,), 0, 6)
    nominal = jnp.right_shift(jnp.full((TOTAL,), longest, jnp.int32), halvings.astype(jnp.int32))
    trimmed = jax.random.randint(second_key, (TOTAL,), 0, 1 << 20) % jnp.maximum(nominal // 2, 1)
    lengths = jnp.maximum(nominal - trimmed, 1).astype(jnp.int32)
    user_ends = jnp.cumsum(lengths).astype(jnp.int32)
    user_starts = user_ends - lengths
    indices_all = jnp.arange(TOTAL, dtype=jnp.int32)
    owners = jnp.searchsorted(user_ends, indices_all, side='right').astype(jnp.int32)
    head_first = user_starts[owners]
    head_last = jnp.minimum(user_ends[owners] - 1, cut_row - 1)
    tail_first = jnp.where(indices_all == TOTAL - 1, TOTAL - 1, cut_row).astype(jnp.int32)
    tail_last = jnp.where(indices_all == TOTAL - 1, TOTAL - 1, TOTAL - 2).astype(jnp.int32)
    in_head = indices_all < cut_row
    first_rows = jnp.where(in_head, head_first, tail_first)
    last_rows = jnp.where(in_head, head_last, tail_last)
    return jnp.stack([first_rows, last_rows]).astype(jnp.int32)


def draw_value_vectors(key, part):
    columns_all = HEADS * DH
    first_key, second_key, third_key = jax.random.split(jax.random.fold_in(key, 11), 3)
    head_ids = jnp.arange(columns_all, dtype=jnp.int32) // DH
    rising = 3.0 ** (head_ids.astype(jnp.float32) / max(HEADS - 1, 1))
    column_scale = jnp.exp(jax.random.uniform(first_key, (columns_all,), jnp.float32, 0.0, math.log(10.0)))
    row_scale = jnp.exp(jax.random.uniform(second_key, (TOTAL, 1), jnp.float32, 0.0, math.log(10.0)))
    spread = rising[None, :] * column_scale[None, :] * row_scale / 10.0
    entries = jnp.clip(jax.random.normal(third_key, (TOTAL, columns_all), jnp.float32), -4.0, 4.0)
    return (entries * spread).astype(jnp.bfloat16)


def steps_of(key, extent, cuts, low, largest):
    def one(position, parts):
        heights = jax.random.uniform(jax.random.fold_in(jax.random.fold_in(key, 6), position), (parts,), jnp.float32, low / len(cuts), largest / len(cuts))
        return jnp.repeat(jnp.exp(heights), extent[position] // parts).reshape((-1,) + (1,) * (len(extent) - position - 1))

    level = one(*cuts[0])
    for cut in cuts[1:]:
        level = level * one(*cut)
    return level


def centred(key, extent, scale, bound, shards=(), kind=jnp.bfloat16):
    loudness = steps_of(key, extent, shards, -0.22, 0.18) if shards else 1.0
    values = jax.random.normal(key, extent, jnp.float32) * scale * loudness
    return jnp.minimum(jnp.maximum(values, -bound), bound).astype(kind)


def setup_inputs(seed: int = 0) -> dict:
    arg_keys = jax.random.split(jax.random.key(seed), 7)
    return {
        "queries": centred(arg_keys[0], (TOTAL, HEADS * DH), 1.0, 6.0, ((0, 8), (1, 4))),
        "key_vectors": centred(arg_keys[1], (TOTAL, HEADS * DH), 1.0, 6.0, ((0, 8), (1, 4))),
        "value_vectors": draw_value_vectors(jax.random.fold_in(arg_keys[6], 71), 0),
        "gating": centred(arg_keys[3], (TOTAL, HEADS * DH), 1.0, 6.0, ((0, 8), (1, 4))),
        "bounds": draw_bounds(jax.random.fold_in(arg_keys[6], 71), 0),
        "cotangent": centred(arg_keys[5], (TOTAL, HEADS * DH), 1.0, 6.0, ((0, 8), (1, 4))),
    }


EPSILON = 1e-05

def silu_parts(query_tile, key_tile, allowed, factor):
    scores = jnp.einsum('qhd,khd->hqk', query_tile.astype(jnp.float32), key_tile.astype(jnp.float32)) * factor
    sigmoid = jax.nn.sigmoid(scores)
    weights = jnp.where(allowed[None], scores * sigmoid, 0.0).astype(jnp.bfloat16)
    return (scores, sigmoid, weights)

def reference(queries, key_vectors, value_vectors, gating, bounds, cotangent):
    factor = DH ** (-0.5)
    margin = REACH * ROWS_DEV
    window_size = (REACH + 1) * ROWS_DEV
    block_count = TOTAL // ROWS_DEV
    features = HEADS * DH
    query_all = queries.reshape(TOTAL, HEADS, DH)
    key_pad = jnp.concatenate([jnp.zeros((margin, HEADS, DH), key_vectors.dtype), key_vectors.reshape(TOTAL, HEADS, DH)], 0)
    value_pad = jnp.concatenate([jnp.zeros((margin, HEADS, DH), value_vectors.dtype), value_vectors.reshape(TOTAL, HEADS, DH)], 0)
    first_rows = bounds[0]
    local_rows = jnp.arange(ROWS_DEV, dtype=jnp.int32)
    window_rows = jnp.arange(window_size, dtype=jnp.int32)

    def tile_inputs(tile_index):
        begin_row = tile_index * ROWS_DEV
        query_tile = lax.dynamic_slice_in_dim(query_all, begin_row, ROWS_DEV, 0)
        key_tile = lax.dynamic_slice_in_dim(key_pad, begin_row, window_size, 0)
        value_tile = lax.dynamic_slice_in_dim(value_pad, begin_row, window_size, 0)
        starts = lax.dynamic_slice_in_dim(first_rows, begin_row, ROWS_DEV, 0)
        row_ids = begin_row + local_rows
        key_ids = begin_row - margin + window_rows
        allowed = (key_ids[None, :] >= starts[:, None]) & (key_ids[None, :] <= row_ids[:, None])
        return (query_tile, key_tile, value_tile, allowed)

    def forward_block(tile_index):
        query_tile, key_tile, value_tile, allowed = tile_inputs(tile_index)
        weights = silu_parts(query_tile, key_tile, allowed, factor)[2]
        return jnp.einsum('hqk,khd->qhd', weights.astype(jnp.float32), value_tile.astype(jnp.float32))
    tile_indices = jnp.arange(block_count, dtype=jnp.int32)
    attended = lax.map(forward_block, tile_indices).reshape(TOTAL, features)
    total_sum = lax.optimization_barrier(jnp.sum(attended, axis=1, keepdims=True))
    square_sum = lax.optimization_barrier(jnp.sum(attended * attended, axis=1, keepdims=True))
    average = total_sum / features
    variance = square_sum / features - average * average
    inverse = lax.rsqrt(variance + EPSILON)
    normed = (attended - average) * inverse
    gate_float = gating.astype(jnp.float32)
    layer_out = (normed * gate_float).astype(jnp.bfloat16)
    upstream = cotangent.astype(jnp.float32)
    grad_gating = (upstream * normed).astype(jnp.bfloat16)
    scaled = upstream * gate_float
    grad_sum = lax.optimization_barrier(jnp.sum(scaled, axis=1, keepdims=True))
    cross_sum = lax.optimization_barrier(jnp.sum(scaled * normed, axis=1, keepdims=True))
    delta_rows = (inverse * (scaled - grad_sum / features - normed * (cross_sum / features))).astype(jnp.bfloat16)
    delta_all = delta_rows.reshape(TOTAL, HEADS, DH)

    def backward_block(accumulated, tile_index):
        grad_key_pad, grad_value_pad = accumulated
        query_tile, key_tile, value_tile, allowed = tile_inputs(tile_index)
        scores, sigmoid, weights = silu_parts(query_tile, key_tile, allowed, factor)
        begin_row = tile_index * ROWS_DEV
        delta_tile = lax.dynamic_slice_in_dim(delta_all, begin_row, ROWS_DEV, 0)
        pulled = jnp.einsum('qhd,khd->hqk', delta_tile.astype(jnp.float32), value_tile.astype(jnp.float32))
        score_grad = jnp.where(allowed[None], pulled * sigmoid * (1.0 + scores * (1.0 - sigmoid)), 0.0).astype(jnp.bfloat16)
        grad_query = (jnp.einsum('hqk,khd->qhd', score_grad.astype(jnp.float32), key_tile.astype(jnp.float32)) * factor).astype(jnp.bfloat16)
        key_add = jnp.einsum('hqk,qhd->khd', score_grad.astype(jnp.float32), query_tile.astype(jnp.float32)) * factor
        value_add = jnp.einsum('hqk,qhd->khd', weights.astype(jnp.float32), delta_tile.astype(jnp.float32))
        grad_key_pad = lax.dynamic_update_slice_in_dim(grad_key_pad, lax.dynamic_slice_in_dim(grad_key_pad, begin_row, window_size, 0) + key_add, begin_row, 0)
        grad_value_pad = lax.dynamic_update_slice_in_dim(grad_value_pad, lax.dynamic_slice_in_dim(grad_value_pad, begin_row, window_size, 0) + value_add, begin_row, 0)
        return ((grad_key_pad, grad_value_pad), grad_query)
    empty_pad = jnp.zeros((TOTAL + margin, HEADS, DH), jnp.float32)
    sums_final, grad_blocks = lax.scan(backward_block, (empty_pad, empty_pad), tile_indices)
    grad_queries = grad_blocks.reshape(TOTAL, features)
    grad_keys = sums_final[0][margin:].reshape(TOTAL, features).astype(jnp.bfloat16)
    grad_values = sums_final[1][margin:].reshape(TOTAL, features).astype(jnp.bfloat16)
    return (layer_out, grad_queries, grad_keys, grad_values, grad_gating)
```

```python
import functools

import jax
import jax.numpy as jnp
from jax import lax
from jax.experimental import pallas as pl
from jax.experimental.pallas import tpu as pltpu
from jax.sharding import PartitionSpec as P

DH = 128
REACH = 2
EPSILON = 1e-05
VMEM_LIMIT = 48 * 1024 * 1024

NT = (((1,), (1,)), ((), ()))
NN = (((1,), (0,)), ((), ()))


def dot(left, right, dims):
    return lax.dot_general(left, right, dims, preferred_element_type=jnp.float32)


def column(row, width):
    return jnp.transpose(jnp.broadcast_to(row, (width, row.shape[1])))


def lane_sums(values):
    ones = jnp.ones((8, values.shape[1]), jnp.float32)
    return lax.dot_general(
        ones, values, NT, precision=lax.Precision.HIGHEST, preferred_element_type=jnp.float32
    )[:1]


def chunk_of(rows):
    return 256 if rows % 256 == 0 else rows


def key_chunks(offset, chunk, chunks):
    if offset == 0:
        return range(chunk + 1)
    if offset == REACH:
        return range(chunk, chunks)
    return range(chunks)


def query_mask(start, rows, size, offset, chunk, other):
    keys = lax.broadcasted_iota(jnp.int32, (size, size), 1) + (other * size - offset * rows)
    mask = keys.astype(jnp.float32) >= start
    if offset == 0 and other == chunk:
        queries = lax.broadcasted_iota(jnp.int32, (size, size), 0) + chunk * size
        mask = mask & (keys <= queries)
    return mask


def key_mask(last, rows, size, offset, chunk, other):
    queries = lax.broadcasted_iota(jnp.int32, (size, size), 1) + (chunk * size + offset * rows)
    mask = queries.astype(jnp.float32) <= last
    if offset == 0 and other == chunk:
        keys = lax.broadcasted_iota(jnp.int32, (size, size), 0) + other * size
        mask = mask & (keys <= queries)
    return mask


def forward_kernel(factor, start_ref, gate_ref, up_ref, q_ref, *refs):
    kv = refs[: 2 * (REACH + 1)]
    att_ref, stats_ref = refs[2 * (REACH + 1) :]
    rows, features = q_ref.shape
    size = chunk_of(rows)
    chunks = rows // size
    starts = column(start_ref[...], size)
    for head in range(features // DH):
        lanes = slice(head * DH, head * DH + DH)
        for chunk in range(chunks):
            here = slice(chunk * size, chunk * size + size)
            query = q_ref[here, lanes]
            total = jnp.zeros((size, DH), jnp.float32)
            for offset in range(REACH + 1):
                for other in key_chunks(offset, chunk, chunks):
                    there = slice(other * size, other * size + size)
                    scores = dot(query, kv[2 * offset][there, lanes], NT) * factor
                    mask = query_mask(starts[here], rows, size, offset, chunk, other)
                    weights = jnp.where(mask, scores * jax.nn.sigmoid(scores), 0.0)
                    total += dot(weights.astype(jnp.bfloat16), kv[2 * offset + 1][there, lanes], NN)
            att_ref[here, lanes] = total
    att = att_ref[...]
    scaled = up_ref[...].astype(jnp.float32) * gate_ref[...].astype(jnp.float32)
    stats_ref[0:1, :] = lane_sums(att)
    stats_ref[1:2, :] = lane_sums(att * att)
    stats_ref[2:3, :] = lane_sums(scaled)
    stats_ref[3:4, :] = lane_sums(scaled * att)


def delta_kernel(total_features, att_ref, gate_ref, up_ref, stats_ref, out_ref, grad_gate_ref, delta_ref):
    stats = jnp.sum(stats_ref[...], axis=0)
    width = att_ref.shape[1]
    average = stats[0:1] / total_features
    inverse = lax.rsqrt(stats[1:2] / total_features - average * average + EPSILON)
    first = stats[2:3] / total_features
    second = inverse * (stats[3:4] - average * stats[2:3]) / total_features
    average, inverse, first, second = [column(row, width) for row in (average, inverse, first, second)]
    normed = (att_ref[...] - average) * inverse
    gate = gate_ref[...].astype(jnp.float32)
    up = up_ref[...].astype(jnp.float32)
    out_ref[...] = (normed * gate).astype(jnp.bfloat16)
    grad_gate_ref[...] = (up * normed).astype(jnp.bfloat16)
    delta_ref[...] = (inverse * (up * gate - first - normed * second)).astype(jnp.bfloat16)


def near_kernel(factor, start_ref, last_ref, q_ref, d_ref, *refs):
    kv = refs[: 2 * (REACH + 1)]
    gq_ref, gk_ref, gv_ref = refs[2 * (REACH + 1) :]
    rows, features = q_ref.shape
    size = chunk_of(rows)
    chunks = rows // size
    starts = column(start_ref[...], size)
    for head in range(features // DH):
        lanes = slice(head * DH, head * DH + DH)
        for chunk in range(chunks):
            here = slice(chunk * size, chunk * size + size)
            query = q_ref[here, lanes]
            delta = d_ref[here, lanes]
            total = jnp.zeros((size, DH), jnp.float32)
            for offset in range(REACH + 1):
                for other in key_chunks(offset, chunk, chunks):
                    there = slice(other * size, other * size + size)
                    key = kv[2 * offset][there, lanes]
                    scores = dot(query, key, NT) * factor
                    sigmoid = jax.nn.sigmoid(scores)
                    pulled = dot(delta, kv[2 * offset + 1][there, lanes], NT)
                    mask = query_mask(starts[here], rows, size, offset, chunk, other)
                    grad = jnp.where(mask, pulled * sigmoid * (1.0 + scores * (1.0 - sigmoid)), 0.0)
                    total += dot(grad.astype(jnp.bfloat16), key, NN)
            gq_ref[here, lanes] = (total * factor).astype(jnp.bfloat16)
    add_key_side(factor, 0, last_ref, kv[0], kv[1], q_ref, d_ref, None, None, gk_ref, gv_ref)


def add_key_side(factor, offset, last_ref, k_ref, v_ref, q_ref, d_ref, bk_ref, bv_ref, gk_ref, gv_ref):
    rows, features = q_ref.shape
    size = chunk_of(rows)
    chunks = rows // size
    lasts = column(last_ref[...], size)
    for head in range(features // DH):
        lanes = slice(head * DH, head * DH + DH)
        for other in range(chunks):
            there = slice(other * size, other * size + size)
            key = k_ref[there, lanes]
            value = v_ref[there, lanes]
            key_total = jnp.zeros((size, DH), jnp.float32)
            value_total = jnp.zeros((size, DH), jnp.float32)
            for chunk in range(chunks):
                if other not in key_chunks(offset, chunk, chunks):
                    continue
                here = slice(chunk * size, chunk * size + size)
                query = q_ref[here, lanes]
                delta = d_ref[here, lanes]
                scores = dot(key, query, NT) * factor
                sigmoid = jax.nn.sigmoid(scores)
                pulled = dot(value, delta, NT)
                mask = key_mask(lasts[there], rows, size, offset, chunk, other)
                weights = jnp.where(mask, scores * sigmoid, 0.0).astype(jnp.bfloat16)
                grad = jnp.where(mask, pulled * sigmoid * (1.0 + scores * (1.0 - sigmoid)), 0.0)
                key_total += dot(grad.astype(jnp.bfloat16), query, NN)
                value_total += dot(weights, delta, NN)
            if bk_ref is not None:
                key_total += bk_ref[there, lanes]
                value_total += bv_ref[there, lanes]
            gk_ref[there, lanes] = key_total
            gv_ref[there, lanes] = value_total


def far_kernel(factor, last_ref, k_ref, v_ref, bk_ref, bv_ref, *refs):
    qd = refs[: 2 * REACH]
    gk_ref, gv_ref, key_sum, value_sum = refs[2 * REACH :]
    key_sum[...] = bk_ref[...]
    value_sum[...] = bv_ref[...]
    for offset in range(1, REACH + 1):
        add_key_side(
            factor, offset, last_ref, k_ref, v_ref, qd[2 * offset - 2], qd[2 * offset - 1],
            key_sum, value_sum, key_sum, value_sum,
        )
    gk_ref[...] = (key_sum[...] * factor).astype(jnp.bfloat16)
    gv_ref[...] = value_sum[...].astype(jnp.bfloat16)


def call(kernel, outs, *args, scratch=()):
    return pl.pallas_call(
        kernel,
        out_shape=[jax.ShapeDtypeStruct(shape, dtype) for shape, dtype in outs],
        scratch_shapes=list(scratch),
        compiler_params=pltpu.CompilerParams(vmem_limit_bytes=VMEM_LIMIT),
    )(*args)


def shift(value, axis, steps):
    count = lax.axis_size(axis)
    return lax.ppermute(value, axis, [(source, (source + steps) % count) for source in range(count)])


def local(queries, key_vectors, value_vectors, gating, bounds, cotangent):
    block = queries.shape
    rows_dev = block[0]
    factor = DH ** (-0.5)
    heads = lax.axis_size("heads")
    first_row = lax.axis_index("rows") * rows_dev
    relative = (bounds - first_row).astype(jnp.float32)
    start, last = relative[0:1], relative[1:2]

    kv = [key_vectors, value_vectors]
    for offset in range(1, REACH + 1):
        kv += [shift(key_vectors, "rows", offset), shift(value_vectors, "rows", offset)]
    later = [shift(queries, "rows", -offset) for offset in range(1, REACH + 1)]

    attended, stats = call(
        functools.partial(forward_kernel, factor),
        [(block, jnp.float32), ((4, rows_dev), jnp.float32)],
        start, gating, cotangent, queries, *kv,
    )
    stats = jnp.stack([stats] + [shift(stats, "heads", step) for step in range(1, heads)])
    layer_out, grad_gating, delta = call(
        functools.partial(delta_kernel, float(block[1] * heads)),
        [(block, jnp.bfloat16)] * 3,
        attended, gating, cotangent, stats,
    )
    delta_later = [shift(delta, "rows", -offset) for offset in range(1, REACH + 1)]
    grad_queries, grad_key, grad_value = call(
        functools.partial(near_kernel, factor),
        [(block, jnp.bfloat16), (block, jnp.float32), (block, jnp.float32)],
        start, last, queries, delta, *kv,
    )
    pairs = [value for pair in zip(later, delta_later) for value in pair]
    grad_keys, grad_values = call(
        functools.partial(far_kernel, factor),
        [(block, jnp.bfloat16)] * 2,
        last, key_vectors, value_vectors, grad_key, grad_value, *pairs,
        scratch=[pltpu.VMEM(block, jnp.float32)] * 2,
    )
    return (layer_out, grad_queries, grad_keys, grad_values, grad_gating)


def solution(mesh):
    return jax.shard_map(
        local,
        mesh=mesh,
        in_specs=(
            P("rows", "heads"),
            P("rows", "heads"),
            P("rows", "heads"),
            P("rows", "heads"),
            P(None, "rows"),
            P("rows", "heads"),
        ),
        out_specs=(P("rows", "heads"),) * 5,
        check_vma=False,
    )
```

```python
import functools

import jax
import jax.numpy as jnp
from jax import lax
from jax.experimental import pallas as pl
from jax.experimental.pallas import tpu as pltpu
from jax.sharding import PartitionSpec as P

DH = 128
REACH = 2
EPSILON = 1e-05
VMEM_LIMIT = 20 * 1024 * 1024

LANES = 128
NT = (((1,), (1,)), ((), ()))
NN = (((1,), (0,)), ((), ()))


def dot(left, right, dims):
    return lax.dot_general(left, right, dims, preferred_element_type=jnp.float32)


def column(row, width):
    return jnp.transpose(jnp.broadcast_to(row, (width, row.shape[1])))


def lane_sums(values):
    ones = jnp.ones((8, values.shape[1]), jnp.float32)
    return lax.dot_general(
        ones, values, NT, precision=lax.Precision.HIGHEST, preferred_element_type=jnp.float32
    )[:1]


def chunk_of(rows):
    return 256 if rows % 256 == 0 else rows


def query_mask(start, rows, offset, chunk):
    size, width = start.shape
    keys = lax.broadcasted_iota(jnp.int32, (size, width), 1) - offset * rows
    mask = keys.astype(jnp.float32) >= start
    if offset == 0:
        queries = lax.broadcasted_iota(jnp.int32, (size, width), 0) + chunk * size
        mask = mask & (keys <= queries)
    return mask


def key_mask(last, rows, offset, chunk):
    size, width = last.shape
    queries = lax.broadcasted_iota(jnp.int32, (size, width), 1) + offset * rows
    mask = queries.astype(jnp.float32) <= last
    if offset == 0:
        keys = lax.broadcasted_iota(jnp.int32, (size, width), 0) + chunk * size
        mask = mask & (keys <= queries)
    return mask


def silu_and_slope(scores, mask):
    scores = jnp.where(mask, scores, 0.0)
    sigmoid = jax.nn.sigmoid(scores)
    weights = scores * sigmoid
    slope = jnp.where(mask, sigmoid + weights * (1.0 - sigmoid), 0.0)
    return weights.astype(jnp.bfloat16), slope


def parts_of(rows, features):
    size = chunk_of(rows)
    lanes = [(head, slice(head * DH, head * DH + DH)) for head in range(features // DH)]
    chunks = [(chunk, slice(chunk * size, chunk * size + size)) for chunk in range(rows // size)]
    return lanes, chunks


def widen(ref, width):
    return jnp.concatenate([ref[...]] * (width // ref.shape[1]), axis=1)


def column_kernel(row_ref, start_ref, last_ref):
    start_ref[...] = column(row_ref[0:1, :], LANES)
    last_ref[...] = column(row_ref[1:2, :], LANES)


def own_kernel(factor, start_ref, last_ref, q_ref, k_ref, gate_ref, up_ref, *refs):
    weight_ref, slope_ref, weight_t_ref, slope_t_ref, scaled_ref, sum_ref = refs
    rows, features = q_ref.shape
    lanes, chunks = parts_of(rows, features)
    starts = widen(start_ref, rows)
    lasts = widen(last_ref, rows)
    for head, at in lanes:
        for chunk, here in chunks:
            scores = dot(q_ref[here, at], k_ref[:, at], NT) * factor
            weights, slope = silu_and_slope(scores, query_mask(starts[here], rows, 0, chunk))
            weight_ref[head, here, :] = weights
            slope_ref[head, here, :] = slope
            scores = dot(k_ref[here, at], q_ref[:, at], NT) * factor
            weights, slope = silu_and_slope(scores, key_mask(lasts[here], rows, 0, chunk))
            weight_t_ref[head, here, :] = weights
            slope_t_ref[head, here, :] = slope
    scaled = up_ref[...].astype(jnp.float32) * gate_ref[...].astype(jnp.float32)
    scaled_ref[...] = scaled
    sum_ref[...] = lane_sums(scaled)


def weight_kernel(factor, start_ref, q_ref, *refs):
    keys, (weight_ref, slope_ref) = refs[:REACH], refs[REACH:]
    rows, features = q_ref.shape
    lanes, chunks = parts_of(rows, features)
    starts = widen(start_ref, rows)
    for head, at in lanes:
        for chunk, here in chunks:
            for offset in range(1, REACH + 1):
                scores = dot(q_ref[here, at], keys[offset - 1][:, at], NT) * factor
                weights, slope = silu_and_slope(scores, query_mask(starts[here], rows, offset, chunk))
                weight_ref[head, offset - 1, here, :] = weights
                slope_ref[head, offset - 1, here, :] = slope


def later_kernel(factor, last_ref, k_ref, *refs):
    queries, (weight_ref, slope_ref) = refs[:REACH], refs[REACH:]
    rows, features = k_ref.shape
    lanes, chunks = parts_of(rows, features)
    lasts = widen(last_ref, rows)
    for head, at in lanes:
        for chunk, here in chunks:
            for offset in range(1, REACH + 1):
                scores = dot(k_ref[here, at], queries[offset - 1][:, at], NT) * factor
                weights, slope = silu_and_slope(scores, key_mask(lasts[here], rows, offset, chunk))
                weight_ref[head, offset - 1, here, :] = weights
                slope_ref[head, offset - 1, here, :] = slope


def attend_kernel(own_weight_ref, scaled_ref, sum_ref, weight_ref, *refs):
    values, (att_ref, stats_ref) = refs[: REACH + 1], refs[REACH + 1 :]
    rows, features = scaled_ref.shape
    lanes, chunks = parts_of(rows, features)
    for head, at in lanes:
        for chunk, here in chunks:
            total = dot(own_weight_ref[head, here, :], values[0][:, at], NN)
            for offset in range(REACH):
                total += dot(weight_ref[head, offset, here, :], values[offset + 1][:, at], NN)
            att_ref[here, at] = total
    att = att_ref[...]
    stats_ref[0:1, :] = lane_sums(att)
    stats_ref[1:2, :] = lane_sums(att * att)
    stats_ref[2:3, :] = sum_ref[...]
    stats_ref[3:4, :] = lane_sums(scaled_ref[...] * att)


def delta_kernel(total_features, att_ref, scaled_ref, *refs):
    stats_refs, (normed_ref, delta_ref) = refs[:-2], refs[-2:]
    stats = stats_refs[0][...]
    for ref in stats_refs[1:]:
        stats += ref[...]
    width = att_ref.shape[1]
    average = stats[0:1] / total_features
    inverse = lax.rsqrt(stats[1:2] / total_features - average * average + EPSILON)
    first = stats[2:3] / total_features
    second = inverse * (stats[3:4] - average * stats[2:3]) / total_features
    average, inverse, first, second = [column(row, width) for row in (average, inverse, first, second)]
    normed = (att_ref[...] - average) * inverse
    normed_ref[...] = normed
    delta_ref[...] = (inverse * (scaled_ref[...] - first - normed * second)).astype(jnp.bfloat16)


def near_kernel(factor, q_ref, k_ref, v_ref, gate_ref, up_ref, d_ref, normed_ref, own_slope_ref,
                own_weight_t_ref, own_slope_t_ref, slope_ref, *refs):
    keys, values, refs = refs[:REACH], refs[REACH : 2 * REACH], refs[2 * REACH :]
    gq_ref, gk_ref, gv_ref, out_ref, gg_ref = refs
    rows, features = q_ref.shape
    lanes, chunks = parts_of(rows, features)
    normed = normed_ref[...]
    out_ref[...] = (normed * gate_ref[...].astype(jnp.float32)).astype(jnp.bfloat16)
    gg_ref[...] = (normed * up_ref[...].astype(jnp.float32)).astype(jnp.bfloat16)
    for head, at in lanes:
        for chunk, here in chunks:
            delta = d_ref[here, at]
            grad = (dot(delta, v_ref[:, at], NT) * own_slope_ref[head, here, :]).astype(jnp.bfloat16)
            total = dot(grad, k_ref[:, at], NN)
            for offset in range(REACH):
                grad = dot(delta, values[offset][:, at], NT) * slope_ref[head, offset, here, :]
                total += dot(grad.astype(jnp.bfloat16), keys[offset][:, at], NN)
            gq_ref[here, at] = (total * factor).astype(jnp.bfloat16)
            grad = dot(v_ref[here, at], d_ref[:, at], NT) * own_slope_t_ref[head, here, :]
            gk_ref[here, at] = dot(grad.astype(jnp.bfloat16), q_ref[:, at], NN)
            gv_ref[here, at] = dot(own_weight_t_ref[head, here, :], d_ref[:, at], NN)


def far_kernel(factor, v_ref, near_k_ref, near_v_ref, weight_ref, slope_ref, *refs):
    queries, deltas, (gk_ref, gv_ref) = refs[:REACH], refs[REACH : 2 * REACH], refs[2 * REACH :]
    rows, features = v_ref.shape
    lanes, chunks = parts_of(rows, features)
    for head, at in lanes:
        for chunk, here in chunks:
            key_total = near_k_ref[here, at]
            value_total = near_v_ref[here, at]
            for offset in range(REACH):
                delta = deltas[offset][:, at]
                value_total += dot(weight_ref[head, offset, here, :], delta, NN)
                grad = dot(v_ref[here, at], delta, NT) * slope_ref[head, offset, here, :]
                key_total += dot(grad.astype(jnp.bfloat16), queries[offset][:, at], NN)
            gv_ref[here, at] = value_total.astype(jnp.bfloat16)
            gk_ref[here, at] = (key_total * factor).astype(jnp.bfloat16)


def call(kernel, outs, *args, cost=None):
    vmem = pl.BlockSpec(memory_space=pltpu.VMEM)
    return pl.pallas_call(
        kernel,
        out_shape=[jax.ShapeDtypeStruct(shape, dtype) for shape, dtype in outs],
        in_specs=[vmem] * len(args),
        out_specs=[vmem] * len(outs),
        cost_estimate=cost,
        compiler_params=pltpu.CompilerParams(vmem_limit_bytes=VMEM_LIMIT),
    )(*args)


def shift(value, axis, steps, ring=True):
    count = lax.axis_size(axis)
    pairs = [(source, source + steps) for source in range(count)]
    if ring:
        pairs = [(source, target % count) for source, target in pairs]
    return lax.ppermute(value, axis, [(s, t) for s, t in pairs if 0 <= t < count])


def local(queries, key_vectors, value_vectors, gating, bounds, cotangent):
    block = queries.shape
    rows_dev = block[0]
    heads_dev = block[1] // DH
    factor = DH ** (-0.5)
    heads = lax.axis_size("heads")
    first_row = lax.axis_index("rows") * rows_dev
    relative = (bounds - first_row).astype(jnp.float32)
    half, full = jnp.bfloat16, jnp.float32
    square = (rows_dev, rows_dev)
    steps = range(1, REACH + 1)

    keys = [shift(key_vectors, "rows", offset) for offset in steps]
    values = [shift(value_vectors, "rows", offset) for offset in steps]

    starts, lasts = call(
        column_kernel, [((rows_dev, LANES), full)] * 2, relative, cost=pl.CostEstimate(flops=10**10, transcendentals=0, bytes_accessed=4*10**7),
    )
    own = (heads_dev, *square)
    own_weights, own_slopes, own_weights_t, own_slopes_t, scaled, scaled_sum = call(
        functools.partial(own_kernel, factor),
        [(own, half), (own, full), (own, half), (own, full), (block, full), ((1, rows_dev), full)],
        starts, lasts, queries, key_vectors, gating, cotangent,
    )
    pair = (heads_dev, REACH, *square)
    weights, slopes = call(
        functools.partial(weight_kernel, factor), [(pair, half), (pair, full)], starts, queries, *keys
    )
    tied, _ = lax.optimization_barrier((queries, weights))
    later = [shift(queries, "rows", -1), shift(tied, "rows", -2)]
    attended, stats = call(
        attend_kernel,
        [(block, full), ((4, rows_dev), full)],
        own_weights, scaled, scaled_sum, weights, value_vectors, *values,
    )
    weights_t, slopes_t = call(
        functools.partial(later_kernel, factor), [(pair, half), (pair, full)], lasts, key_vectors, *later
    )
    all_stats = [stats] + [shift(stats, "heads", step) for step in range(1, heads)]
    all_stats, weights_t = lax.optimization_barrier((all_stats, weights_t))
    normed, delta = call(
        functools.partial(delta_kernel, float(block[1] * heads)),
        [(block, full), (block, half)],
        attended, scaled, *all_stats,
    )
    deltas = [shift(delta, "rows", -offset) for offset in steps]
    grad_queries, near_key, near_value, layer_out, grad_gating = call(
        functools.partial(near_kernel, factor),
        [(block, half), (block, full), (block, full), (block, half), (block, half)],
        queries, key_vectors, value_vectors, gating, cotangent, delta, normed,
        own_slopes, own_weights_t, own_slopes_t, slopes, *keys, *values,
    )
    grad_keys, grad_values = call(
        functools.partial(far_kernel, factor),
        [(block, half)] * 2,
        value_vectors, near_key, near_value, weights_t, slopes_t, *later, *deltas,
    )
    return (layer_out, grad_queries, grad_keys, grad_values, grad_gating)


def solution(mesh):
    return jax.shard_map(
        local,
        mesh=mesh,
        in_specs=(
            P("rows", "heads"),
            P("rows", "heads"),
            P("rows", "heads"),
            P("rows", "heads"),
            P(None, "rows"),
            P("rows", "heads"),
        ),
        out_specs=(P("rows", "heads"),) * 5,
        check_vma=False,
    )
```

```python
import functools

import jax
import jax.numpy as jnp
from jax import lax
from jax.experimental import pallas as pl
from jax.experimental.pallas import tpu as pltpu
from jax.sharding import PartitionSpec as P

DH = 128
REACH = 2
EPSILON = 1e-05
VMEM_LIMIT = 20 * 1024 * 1024

LANES = 128
NT = (((1,), (1,)), ((), ()))
NN = (((1,), (0,)), ((), ()))


def dot(left, right, dims):
    return lax.dot_general(left, right, dims, preferred_element_type=jnp.float32)


def column(row, width):
    return jnp.transpose(jnp.broadcast_to(row, (width, row.shape[1])))


def lane_sums(values):
    return jnp.sum(jnp.transpose(values), axis=0, keepdims=True)


def chunk_of(rows):
    return 256 if rows % 256 == 0 else rows


def query_mask(start, rows, offset, chunk):
    size, width = start.shape
    keys = lax.broadcasted_iota(jnp.int32, (size, width), 1) - offset * rows
    mask = keys.astype(jnp.float32) >= start
    if offset == 0:
        queries = lax.broadcasted_iota(jnp.int32, (size, width), 0) + chunk * size
        mask = mask & (keys <= queries)
    return mask


def key_mask(last, rows, offset, chunk):
    size, width = last.shape
    queries = lax.broadcasted_iota(jnp.int32, (size, width), 1) + offset * rows
    mask = queries.astype(jnp.float32) <= last
    if offset == 0:
        keys = lax.broadcasted_iota(jnp.int32, (size, width), 0) + chunk * size
        mask = mask & (keys <= queries)
    return mask


def silu_and_slope(scores, mask):
    scores = jnp.where(mask, scores, 0.0)
    sigmoid = jax.nn.sigmoid(scores)
    weights = scores * sigmoid
    slope = jnp.where(mask, sigmoid + weights * (1.0 - sigmoid), 0.0)
    return weights.astype(jnp.bfloat16), slope


def parts_of(rows, features):
    size = chunk_of(rows)
    lanes = [(head, slice(head * DH, head * DH + DH)) for head in range(features // DH)]
    chunks = [(chunk, slice(chunk * size, chunk * size + size)) for chunk in range(rows // size)]
    return lanes, chunks


def widen(ref, width):
    return jnp.concatenate([ref[...]] * (width // ref.shape[1]), axis=1)


def column_kernel(row_ref, start_ref, last_ref):
    start_ref[...] = column(row_ref[0:1, :], LANES)
    last_ref[...] = column(row_ref[1:2, :], LANES)


def own_kernel(factor, start_ref, last_ref, q_ref, k_ref, gate_ref, up_ref, *refs):
    weight_ref, slope_ref, weight_t_ref, slope_t_ref, scaled_ref, sum_ref = refs
    rows, features = q_ref.shape
    lanes, chunks = parts_of(rows, features)
    starts = widen(start_ref, rows)
    lasts = widen(last_ref, rows)
    for head, at in lanes:
        for chunk, here in chunks:
            scores = dot(q_ref[here, at], k_ref[:, at], NT) * factor
            weights, slope = silu_and_slope(scores, query_mask(starts[here], rows, 0, chunk))
            weight_ref[head, here, :] = weights
            slope_ref[head, here, :] = slope
            scores = dot(k_ref[here, at], q_ref[:, at], NT) * factor
            weights, slope = silu_and_slope(scores, key_mask(lasts[here], rows, 0, chunk))
            weight_t_ref[head, here, :] = weights
            slope_t_ref[head, here, :] = slope
    scaled = up_ref[...].astype(jnp.float32) * gate_ref[...].astype(jnp.float32)
    scaled_ref[...] = scaled
    sum_ref[...] = lane_sums(scaled)


def weight_kernel(factor, start_ref, q_ref, *refs):
    keys, (weight_ref, slope_ref) = refs[:REACH], refs[REACH:]
    rows, features = q_ref.shape
    lanes, chunks = parts_of(rows, features)
    starts = widen(start_ref, rows)
    for head, at in lanes:
        for chunk, here in chunks:
            for offset in range(1, REACH + 1):
                scores = dot(q_ref[here, at], keys[offset - 1][:, at], NT) * factor
                weights, slope = silu_and_slope(scores, query_mask(starts[here], rows, offset, chunk))
                weight_ref[head, offset - 1, here, :] = weights
                slope_ref[head, offset - 1, here, :] = slope


def later_kernel(factor, last_ref, k_ref, *refs):
    queries, (weight_ref, slope_ref) = refs[:REACH], refs[REACH:]
    rows, features = k_ref.shape
    lanes, chunks = parts_of(rows, features)
    lasts = widen(last_ref, rows)
    for head, at in lanes:
        for chunk, here in chunks:
            for offset in range(1, REACH + 1):
                scores = dot(k_ref[here, at], queries[offset - 1][:, at], NT) * factor
                weights, slope = silu_and_slope(scores, key_mask(lasts[here], rows, offset, chunk))
                weight_ref[head, offset - 1, here, :] = weights
                slope_ref[head, offset - 1, here, :] = slope


def attend_kernel(own_weight_ref, scaled_ref, sum_ref, weight_ref, *refs):
    values, (att_ref, stats_ref) = refs[: REACH + 1], refs[REACH + 1 :]
    rows, features = scaled_ref.shape
    lanes, chunks = parts_of(rows, features)
    for head, at in lanes:
        for chunk, here in chunks:
            total = dot(own_weight_ref[head, here, : here.stop], values[0][: here.stop, at], NN)
            for offset in range(REACH):
                low = here.start if offset == REACH - 1 else 0
                total += dot(weight_ref[head, offset, here, low:], values[offset + 1][low:, at], NN)
            att_ref[here, at] = total
    att = jnp.transpose(att_ref[...])
    scaled = jnp.transpose(scaled_ref[...])
    stats_ref[0:1, :] = jnp.sum(att, axis=0, keepdims=True)
    stats_ref[1:2, :] = jnp.sum(att * att, axis=0, keepdims=True)
    stats_ref[2:3, :] = sum_ref[...]
    stats_ref[3:4, :] = jnp.sum(scaled * att, axis=0, keepdims=True)


def delta_kernel(total_features, att_ref, scaled_ref, *refs):
    stats_refs, (normed_ref, delta_ref) = refs[:-2], refs[-2:]
    stats = stats_refs[0][...]
    for ref in stats_refs[1:]:
        stats += ref[...]
    width = att_ref.shape[1]
    average = stats[0:1] / total_features
    inverse = lax.rsqrt(stats[1:2] / total_features - average * average + EPSILON)
    first = stats[2:3] / total_features
    second = inverse * (stats[3:4] - average * stats[2:3]) / total_features
    average, inverse, first, second = [column(row, width) for row in (average, inverse, first, second)]
    normed = (att_ref[...] - average) * inverse
    normed_ref[...] = normed
    delta_ref[...] = (inverse * (scaled_ref[...] - first - normed * second)).astype(jnp.bfloat16)


def near_kernel(factor, q_ref, k_ref, v_ref, gate_ref, up_ref, d_ref, normed_ref, own_slope_ref,
                own_weight_t_ref, own_slope_t_ref, slope_ref, *refs):
    keys, values, refs = refs[:REACH], refs[REACH : 2 * REACH], refs[2 * REACH :]
    gq_ref, gk_ref, gv_ref, out_ref, gg_ref = refs
    rows, features = q_ref.shape
    lanes, chunks = parts_of(rows, features)
    normed = normed_ref[...]
    out_ref[...] = (normed * gate_ref[...].astype(jnp.float32)).astype(jnp.bfloat16)
    gg_ref[...] = (normed * up_ref[...].astype(jnp.float32)).astype(jnp.bfloat16)
    for head, at in lanes:
        for chunk, here in chunks:
            delta = d_ref[here, at]
            grad = (dot(delta, v_ref[:, at], NT) * own_slope_ref[head, here, :]).astype(jnp.bfloat16)
            total = dot(grad, k_ref[:, at], NN)
            for offset in range(REACH):
                grad = dot(delta, values[offset][:, at], NT) * slope_ref[head, offset, here, :]
                total += dot(grad.astype(jnp.bfloat16), keys[offset][:, at], NN)
            gq_ref[here, at] = (total * factor).astype(jnp.bfloat16)
            grad = dot(v_ref[here, at], d_ref[:, at], NT) * own_slope_t_ref[head, here, :]
            gk_ref[here, at] = dot(grad.astype(jnp.bfloat16), q_ref[:, at], NN)
            gv_ref[here, at] = dot(own_weight_t_ref[head, here, :], d_ref[:, at], NN)


def far_kernel(factor, v_ref, near_k_ref, near_v_ref, weight_ref, slope_ref, *refs):
    queries, deltas, (gk_ref, gv_ref) = refs[:REACH], refs[REACH : 2 * REACH], refs[2 * REACH :]
    rows, features = v_ref.shape
    lanes, chunks = parts_of(rows, features)
    for head, at in lanes:
        for chunk, here in chunks:
            ends = [here.stop if offset == REACH - 1 else rows for offset in range(REACH)]
            delta = jnp.concatenate([ref[:end, at] for ref, end in zip(deltas, ends)], axis=0)
            query = jnp.concatenate([ref[:end, at] for ref, end in zip(queries, ends)], axis=0)
            slope = jnp.concatenate([slope_ref[head, offset, here, :end] for offset, end in enumerate(ends)], axis=1)
            weight = jnp.concatenate([weight_ref[head, offset, here, :end] for offset, end in enumerate(ends)], axis=1)
            grad = (dot(v_ref[here, at], delta, NT) * slope).astype(jnp.bfloat16)
            gv_ref[here, at] = (near_v_ref[here, at] + dot(weight, delta, NN)).astype(jnp.bfloat16)
            gk_ref[here, at] = ((near_k_ref[here, at] + dot(grad, query, NN)) * factor).astype(jnp.bfloat16)


def call(kernel, outs, *args, cost=None):
    vmem = pl.BlockSpec(memory_space=pltpu.VMEM)
    return pl.pallas_call(
        kernel,
        out_shape=[jax.ShapeDtypeStruct(shape, dtype) for shape, dtype in outs],
        in_specs=[vmem] * len(args),
        out_specs=[vmem] * len(outs),
        cost_estimate=cost,
        compiler_params=pltpu.CompilerParams(vmem_limit_bytes=VMEM_LIMIT),
    )(*args)


def shift(value, axis, steps, ring=True):
    count = lax.axis_size(axis)
    pairs = [(source, source + steps) for source in range(count)]
    if ring:
        pairs = [(source, target % count) for source, target in pairs]
    return lax.ppermute(value, axis, [(s, t) for s, t in pairs if 0 <= t < count])


def meet(value, axis, step):
    count = lax.axis_size(axis)
    if count & (count - 1):
        return shift(value, axis, step)
    return lax.ppermute(value, axis, [(source, source ^ step) for source in range(count)])


def local(queries, key_vectors, value_vectors, gating, bounds, cotangent):
    block = queries.shape
    rows_dev = block[0]
    heads_dev = block[1] // DH
    factor = DH ** (-0.5)
    heads = lax.axis_size("heads")
    first_row = lax.axis_index("rows") * rows_dev
    relative = (bounds - first_row).astype(jnp.float32)
    half, full = jnp.bfloat16, jnp.float32
    square = (rows_dev, rows_dev)
    steps = range(1, REACH + 1)

    keys = [shift(key_vectors, "rows", offset) for offset in steps]
    values = [shift(value_vectors, "rows", offset) for offset in steps]

    starts, lasts = call(
        column_kernel, [((rows_dev, LANES), full)] * 2, relative, cost=pl.CostEstimate(flops=10**10, transcendentals=0, bytes_accessed=4*10**7),
    )
    own = (heads_dev, *square)
    own_weights, own_slopes, own_weights_t, own_slopes_t, scaled, scaled_sum = call(
        functools.partial(own_kernel, factor),
        [(own, half), (own, full), (own, half), (own, full), (block, full), ((1, rows_dev), full)],
        starts, lasts, queries, key_vectors, gating, cotangent,
    )
    pair = (heads_dev, REACH, *square)
    weights, slopes = call(
        functools.partial(weight_kernel, factor), [(pair, half), (pair, full)], starts, queries, *keys
    )
    tied, _ = lax.optimization_barrier((queries, weights))
    later = [shift(queries, "rows", -1), shift(tied, "rows", -2)]
    attended, stats = call(
        attend_kernel,
        [(block, full), ((4, rows_dev), full)],
        own_weights, scaled, scaled_sum, weights, value_vectors, *values,
    )
    weights_t, slopes_t = call(
        functools.partial(later_kernel, factor), [(pair, half), (pair, full)], lasts, key_vectors, *later
    )
    all_stats = [stats] + [meet(stats, "heads", step) for step in reversed(range(1, heads))]
    all_stats, weights_t = lax.optimization_barrier((all_stats, weights_t))
    normed, delta = call(
        functools.partial(delta_kernel, float(block[1] * heads)),
        [(block, full), (block, half)],
        attended, scaled, *all_stats,
    )
    deltas = [shift(delta, "rows", -offset) for offset in steps]
    grad_queries, near_key, near_value, layer_out, grad_gating = call(
        functools.partial(near_kernel, factor),
        [(block, half), (block, full), (block, full), (block, half), (block, half)],
        queries, key_vectors, value_vectors, gating, cotangent, delta, normed,
        own_slopes, own_weights_t, own_slopes_t, slopes, *keys, *values,
    )
    grad_keys, grad_values = call(
        functools.partial(far_kernel, factor),
        [(block, half)] * 2,
        value_vectors, near_key, near_value, weights_t, slopes_t, *later, *deltas,
    )
    return (layer_out, grad_queries, grad_keys, grad_values, grad_gating)


def solution(mesh):
    return jax.shard_map(
        local,
        mesh=mesh,
        in_specs=(
            P("rows", "heads"),
            P("rows", "heads"),
            P("rows", "heads"),
            P("rows", "heads"),
            P(None, "rows"),
            P("rows", "heads"),
        ),
        out_specs=(P("rows", "heads"),) * 5,
        check_vma=False,
    )
```

```python
import functools

import jax
import jax.numpy as jnp
from jax import lax
from jax.experimental import pallas as pl
from jax.experimental.pallas import tpu as pltpu
from jax.sharding import PartitionSpec as P

DH = 128
REACH = 2
EPSILON = 1e-05
VMEM_LIMIT = 20 * 1024 * 1024

LANES = 128
NT = (((1,), (1,)), ((), ()))
NN = (((1,), (0,)), ((), ()))


def dot(left, right, dims):
    return lax.dot_general(left, right, dims, preferred_element_type=jnp.float32)


def column(row, width):
    return jnp.transpose(jnp.broadcast_to(row, (width, row.shape[1])))


def lane_sums(values):
    return jnp.sum(jnp.transpose(values), axis=0, keepdims=True)


def chunk_of(rows):
    return 256 if rows % 256 == 0 else rows


def query_mask(start, rows, offset, chunk):
    size, width = start.shape
    keys = lax.broadcasted_iota(jnp.int32, (size, width), 1) - offset * rows
    mask = keys.astype(jnp.float32) >= start
    if offset == 0:
        queries = lax.broadcasted_iota(jnp.int32, (size, width), 0) + chunk * size
        mask = mask & (keys <= queries)
    return mask


def key_mask(last, rows, offset, chunk):
    size, width = last.shape
    queries = lax.broadcasted_iota(jnp.int32, (size, width), 1) + offset * rows
    mask = queries.astype(jnp.float32) <= last
    if offset == 0:
        keys = lax.broadcasted_iota(jnp.int32, (size, width), 0) + chunk * size
        mask = mask & (keys <= queries)
    return mask


def silu_and_slope(scores, mask):
    scores = jnp.where(mask, scores, 0.0)
    sigmoid = jax.nn.sigmoid(scores)
    weights = scores * sigmoid
    slope = jnp.where(mask, sigmoid + weights * (1.0 - sigmoid), 0.0)
    return weights.astype(jnp.bfloat16), slope


def parts_of(rows, features):
    size = chunk_of(rows)
    lanes = [(head, slice(head * DH, head * DH + DH)) for head in range(features // DH)]
    chunks = [(chunk, slice(chunk * size, chunk * size + size)) for chunk in range(rows // size)]
    return lanes, chunks


def widen(ref, width):
    return jnp.concatenate([ref[...]] * (width // ref.shape[1]), axis=1)


def column_kernel(row_ref, start_ref, last_ref):
    start_ref[...] = column(row_ref[0:1, :], LANES)
    last_ref[...] = column(row_ref[1:2, :], LANES)


def own_kernel(factor, start_ref, last_ref, q_ref, k_ref, gate_ref, up_ref, *refs):
    weight_ref, slope_ref, weight_t_ref, slope_t_ref, scaled_ref, sum_ref = refs
    rows, features = q_ref.shape
    lanes, chunks = parts_of(rows, features)
    starts = widen(start_ref, rows)
    lasts = widen(last_ref, rows)
    for head, at in lanes:
        for chunk, here in chunks:
            scores = dot(q_ref[here, at], k_ref[:, at], NT) * factor
            weights, slope = silu_and_slope(scores, query_mask(starts[here], rows, 0, chunk))
            weight_ref[head, here, :] = weights
            slope_ref[head, here, :] = slope
            scores = dot(k_ref[here, at], q_ref[:, at], NT) * factor
            weights, slope = silu_and_slope(scores, key_mask(lasts[here], rows, 0, chunk))
            weight_t_ref[head, here, :] = weights
            slope_t_ref[head, here, :] = slope
    scaled = up_ref[...].astype(jnp.float32) * gate_ref[...].astype(jnp.float32)
    scaled_ref[...] = scaled
    sum_ref[...] = lane_sums(scaled)


def weight_kernel(factor, start_ref, q_ref, *refs):
    keys, (weight_ref, slope_ref) = refs[:REACH], refs[REACH:]
    rows, features = q_ref.shape
    lanes, chunks = parts_of(rows, features)
    starts = widen(start_ref, rows)
    for head, at in lanes:
        for chunk, here in chunks:
            for offset in range(1, REACH + 1):
                scores = dot(q_ref[here, at], keys[offset - 1][:, at], NT) * factor
                weights, slope = silu_and_slope(scores, query_mask(starts[here], rows, offset, chunk))
                weight_ref[head, offset - 1, here, :] = weights
                slope_ref[head, offset - 1, here, :] = slope


def later_kernel(factor, last_ref, k_ref, *refs):
    queries, (weight_ref, slope_ref) = refs[:REACH], refs[REACH:]
    rows, features = k_ref.shape
    lanes, chunks = parts_of(rows, features)
    lasts = widen(last_ref, rows)
    for head, at in lanes:
        for chunk, here in chunks:
            for offset in range(1, REACH + 1):
                scores = dot(k_ref[here, at], queries[offset - 1][:, at], NT) * factor
                weights, slope = silu_and_slope(scores, key_mask(lasts[here], rows, offset, chunk))
                weight_ref[head, offset - 1, here, :] = weights
                slope_ref[head, offset - 1, here, :] = slope


def attend_kernel(own_weight_ref, scaled_ref, sum_ref, weight_ref, *refs):
    values, (att_ref, stats_ref) = refs[: REACH + 1], refs[REACH + 1 :]
    rows, features = scaled_ref.shape
    lanes, chunks = parts_of(rows, features)
    for head, at in lanes:
        for chunk, here in chunks:
            total = dot(own_weight_ref[head, here, : here.stop], values[0][: here.stop, at], NN)
            for offset in range(REACH):
                low = here.start if offset == REACH - 1 else 0
                total += dot(weight_ref[head, offset, here, low:], values[offset + 1][low:, at], NN)
            att_ref[here, at] = total
    att = jnp.transpose(att_ref[...])
    scaled = jnp.transpose(scaled_ref[...])
    stats_ref[0:1, :] = jnp.sum(att, axis=0, keepdims=True)
    stats_ref[1:2, :] = jnp.sum(att * att, axis=0, keepdims=True)
    stats_ref[2:3, :] = sum_ref[...]
    stats_ref[3:4, :] = jnp.sum(scaled * att, axis=0, keepdims=True)


def delta_kernel(total_features, att_ref, scaled_ref, *refs):
    stats_refs, (normed_ref, delta_ref) = refs[:-2], refs[-2:]
    stats = stats_refs[0][...]
    for ref in stats_refs[1:]:
        stats += ref[...]
    width = att_ref.shape[1]
    average = stats[0:1] / total_features
    inverse = lax.rsqrt(stats[1:2] / total_features - average * average + EPSILON)
    first = stats[2:3] / total_features
    second = inverse * (stats[3:4] - average * stats[2:3]) / total_features
    average, inverse, first, second = [column(row, width) for row in (average, inverse, first, second)]
    normed = (att_ref[...] - average) * inverse
    normed_ref[...] = normed
    delta_ref[...] = (inverse * (scaled_ref[...] - first - normed * second)).astype(jnp.bfloat16)


def near_kernel(factor, q_ref, k_ref, v_ref, gate_ref, up_ref, d_ref, normed_ref, own_slope_ref,
                own_weight_t_ref, own_slope_t_ref, slope_ref, *refs):
    keys, values, refs = refs[:REACH], refs[REACH : 2 * REACH], refs[2 * REACH :]
    gq_ref, gk_ref, gv_ref, out_ref, gg_ref = refs
    rows, features = q_ref.shape
    lanes, chunks = parts_of(rows, features)
    normed = normed_ref[...]
    out_ref[...] = (normed * gate_ref[...].astype(jnp.float32)).astype(jnp.bfloat16)
    gg_ref[...] = (normed * up_ref[...].astype(jnp.float32)).astype(jnp.bfloat16)
    for head, at in lanes:
        for chunk, here in chunks:
            delta = d_ref[here, at]
            grad = (dot(delta, v_ref[:, at], NT) * own_slope_ref[head, here, :]).astype(jnp.bfloat16)
            total = dot(grad, k_ref[:, at], NN)
            for offset in range(REACH):
                grad = dot(delta, values[offset][:, at], NT) * slope_ref[head, offset, here, :]
                total += dot(grad.astype(jnp.bfloat16), keys[offset][:, at], NN)
            gq_ref[here, at] = (total * factor).astype(jnp.bfloat16)
            grad = dot(v_ref[here, at], d_ref[:, at], NT) * own_slope_t_ref[head, here, :]
            gk_ref[here, at] = dot(grad.astype(jnp.bfloat16), q_ref[:, at], NN)
            gv_ref[here, at] = dot(own_weight_t_ref[head, here, :], d_ref[:, at], NN)


def far_kernel(factor, reach, v_ref, near_k_ref, near_v_ref, weight_ref, slope_ref, query_ref, d_ref, gk_ref, gv_ref):
    rows, features = v_ref.shape
    lanes, chunks = parts_of(rows, features)
    last = reach == 1
    for head, at in lanes:
        for chunk, here in chunks:
            end = here.stop if reach == REACH else rows
            delta = d_ref[:end, at]
            value = near_v_ref[here, at] + dot(weight_ref[head, reach - 1, here, :end], delta, NN)
            grad = dot(v_ref[here, at], delta, NT) * slope_ref[head, reach - 1, here, :end]
            key = near_k_ref[here, at] + dot(grad.astype(jnp.bfloat16), query_ref[:end, at], NN)
            gv_ref[here, at] = value.astype(gv_ref.dtype)
            gk_ref[here, at] = (key * factor if last else key).astype(gk_ref.dtype)


def call(kernel, outs, *args, cost=None):
    vmem = pl.BlockSpec(memory_space=pltpu.VMEM)
    return pl.pallas_call(
        kernel,
        out_shape=[jax.ShapeDtypeStruct(shape, dtype) for shape, dtype in outs],
        in_specs=[vmem] * len(args),
        out_specs=[vmem] * len(outs),
        cost_estimate=cost,
        compiler_params=pltpu.CompilerParams(vmem_limit_bytes=VMEM_LIMIT),
    )(*args)


def shift(value, axis, steps, around=True):
    count = lax.axis_size(axis)
    pairs = [(source, source + steps) for source in range(count)]
    pairs = [(source, target % count) for source, target in pairs if around or 0 <= target < count]
    return lax.ppermute(value, axis, pairs)


def meet(value, axis, step):
    count = lax.axis_size(axis)
    if count & (count - 1):
        return shift(value, axis, step)
    return lax.ppermute(value, axis, [(source, source ^ step) for source in range(count)])


def local(queries, key_vectors, value_vectors, gating, bounds, cotangent):
    block = queries.shape
    rows_dev = block[0]
    heads_dev = block[1] // DH
    factor = DH ** (-0.5)
    heads = lax.axis_size("heads")
    first_row = lax.axis_index("rows") * rows_dev
    relative = (bounds - first_row).astype(jnp.float32)
    half, full = jnp.bfloat16, jnp.float32
    square = (rows_dev, rows_dev)
    steps = range(1, REACH + 1)

    keys = [shift(key_vectors, "rows", 1), shift(key_vectors, "rows", 2)]
    values = [shift(value_vectors, "rows", 1), shift(value_vectors, "rows", 2)]

    starts, lasts = call(
        column_kernel, [((rows_dev, LANES), full)] * 2, relative, cost=pl.CostEstimate(flops=10**10, transcendentals=0, bytes_accessed=4*10**7),
    )
    own = (heads_dev, *square)
    own_weights, own_slopes, own_weights_t, own_slopes_t, scaled, scaled_sum = call(
        functools.partial(own_kernel, factor),
        [(own, half), (own, full), (own, half), (own, full), (block, full), ((1, rows_dev), full)],
        starts, lasts, queries, key_vectors, gating, cotangent,
    )
    pair = (heads_dev, REACH, *square)
    weights, slopes = call(
        functools.partial(weight_kernel, factor), [(pair, half), (pair, full)], starts, queries, *keys
    )
    tied, _ = lax.optimization_barrier((queries, weights))
    later = [shift(queries, "rows", -1), shift(tied, "rows", -2, around=False)]
    attended, stats = call(
        attend_kernel,
        [(block, full), ((4, rows_dev), full)],
        own_weights, scaled, scaled_sum, weights, value_vectors, *values,
    )
    weights_t, slopes_t = call(
        functools.partial(later_kernel, factor), [(pair, half), (pair, full)], lasts, key_vectors, *later
    )
    all_stats = [stats] + [meet(stats, "heads", step) for step in reversed(range(1, heads))]
    all_stats, weights_t = lax.optimization_barrier((all_stats, weights_t))
    normed, delta = call(
        functools.partial(delta_kernel, float(block[1] * heads)),
        [(block, full), (block, half)],
        attended, scaled, *all_stats,
    )
    deltas = [shift(delta, "rows", -1), shift(delta, "rows", -2)]
    grad_queries, near_key, near_value, layer_out, grad_gating = call(
        functools.partial(near_kernel, factor),
        [(block, half), (block, full), (block, full), (block, half), (block, half)],
        queries, key_vectors, value_vectors, gating, cotangent, delta, normed,
        own_slopes, own_weights_t, own_slopes_t, slopes, *keys, *values,
    )
    sums = [near_key, near_value]
    for offset in reversed(steps):
        sums = call(
            functools.partial(far_kernel, factor, offset),
            [(block, half if offset == 1 else full)] * 2,
            value_vectors, *sums, weights_t, slopes_t, later[offset - 1], deltas[offset - 1],
        )
    grad_keys, grad_values = sums
    return (layer_out, grad_queries, grad_keys, grad_values, grad_gating)


def solution(mesh):
    return jax.shard_map(
        local,
        mesh=mesh,
        in_specs=(
            P("rows", "heads"),
            P("rows", "heads"),
            P("rows", "heads"),
            P("rows", "heads"),
            P(None, "rows"),
            P("rows", "heads"),
        ),
        out_specs=(P("rows", "heads"),) * 5,
        check_vma=False,
    )
```

```python
import functools

import jax
import jax.numpy as jnp
from jax import lax
from jax.experimental import pallas as pl
from jax.experimental.pallas import tpu as pltpu
from jax.sharding import PartitionSpec as P

DH = 128
REACH = 2
EPSILON = 1e-05
VMEM_LIMIT = 20 * 1024 * 1024

LANES = 128
HINT = pl.CostEstimate(flops=10**10, transcendentals=0, bytes_accessed=4 * 10**7)
NT = (((1,), (1,)), ((), ()))
NN = (((1,), (0,)), ((), ()))


def dot(left, right, dims):
    return lax.dot_general(left, right, dims, preferred_element_type=jnp.float32)


def column(row, width):
    return jnp.transpose(jnp.broadcast_to(row, (width, row.shape[1])))


def lane_sums(values):
    return jnp.sum(jnp.transpose(values), axis=0, keepdims=True)


def chunk_of(rows):
    return 256 if rows % 256 == 0 else rows


def query_mask(start, rows, offset, order=None):
    keys = (lax.broadcasted_iota(jnp.int32, start.shape, 1) - offset * rows).astype(jnp.float32)
    mask = keys >= start
    if offset == 0:
        mask = mask & (keys <= order)
    return mask


def key_mask(last, rows, offset, chunk):
    size, width = last.shape
    queries = lax.broadcasted_iota(jnp.int32, (size, width), 1) + offset * rows
    mask = queries.astype(jnp.float32) <= last
    if offset == 0:
        keys = lax.broadcasted_iota(jnp.int32, (size, width), 0) + chunk * size
        mask = mask & (keys <= queries)
    return mask


def silu_and_slope(scores, mask):
    scores = jnp.where(mask, scores, 0.0)
    sigmoid = jax.nn.sigmoid(scores)
    weights = scores * sigmoid
    slope = jnp.where(mask, sigmoid + weights * (1.0 - sigmoid), 0.0)
    return weights.astype(jnp.bfloat16), slope


def parts_of(rows, features):
    size = chunk_of(rows)
    lanes = [(head, slice(head * DH, head * DH + DH)) for head in range(features // DH)]
    chunks = [(chunk, slice(chunk * size, chunk * size + size)) for chunk in range(rows // size)]
    return lanes, chunks


def widen(ref, width):
    return jnp.concatenate([ref[...]] * (width // ref.shape[1]), axis=1)


def order_kernel(order_ref):
    order_ref[...] = lax.broadcasted_iota(jnp.int32, order_ref.shape, 0).astype(jnp.float32)


def column_kernel(row_ref, start_ref, last_ref):
    start_ref[...] = column(row_ref[0:1, :], LANES)
    last_ref[...] = column(row_ref[1:2, :], LANES)


def own_kernel(factor, order_ref, start_ref, last_ref, q_ref, k_ref, gate_ref, up_ref, *refs):
    weight_ref, slope_ref, weight_t_ref, slope_t_ref, scaled_ref, sum_ref = refs
    rows, features = q_ref.shape
    lanes, chunks = parts_of(rows, features)
    starts = widen(start_ref, rows)
    lasts = widen(last_ref, rows)
    for head, at in lanes:
        for chunk, here in chunks:
            scores = dot(q_ref[here, at], k_ref[:, at], NT) * factor
            weights, slope = silu_and_slope(scores, query_mask(starts[here], rows, 0, widen(order_ref, rows)[here]))
            weight_ref[head, here, :] = weights
            slope_ref[head, here, :] = slope
            scores = dot(k_ref[here, at], q_ref[:, at], NT) * factor
            weights, slope = silu_and_slope(scores, key_mask(lasts[here], rows, 0, chunk))
            weight_t_ref[head, here, :] = weights
            slope_t_ref[head, here, :] = slope
    scaled = up_ref[...].astype(jnp.float32) * gate_ref[...].astype(jnp.float32)
    scaled_ref[...] = scaled
    sum_ref[...] = lane_sums(scaled)


def weight_kernel(factor, start_ref, q_ref, *refs):
    keys, (weight_ref, slope_ref) = refs[:REACH], refs[REACH:]
    rows, features = q_ref.shape
    lanes, chunks = parts_of(rows, features)
    starts = widen(start_ref, rows)
    for head, at in lanes:
        for chunk, here in chunks:
            for offset in range(1, REACH + 1):
                scores = dot(q_ref[here, at], keys[offset - 1][:, at], NT) * factor
                weights, slope = silu_and_slope(scores, query_mask(starts[here], rows, offset))
                weight_ref[head, offset - 1, here, :] = weights
                slope_ref[head, offset - 1, here, :] = slope


def later_kernel(factor, *refs):
    flags, (last_ref, k_ref, *refs) = refs[:REACH], refs[REACH:]
    taken, (weight_ref, slope_ref, *queries) = refs[: 2 * REACH], refs[2 * REACH :]
    sort_blocks(flags, taken, queries, False)
    rows, features = k_ref.shape
    lanes, chunks = parts_of(rows, features)
    lasts = widen(last_ref, rows)
    for head, at in lanes:
        for chunk, here in chunks:
            for offset in range(1, REACH + 1):
                scores = dot(k_ref[here, at], queries[offset - 1][:, at], NT) * factor
                weights, slope = silu_and_slope(scores, key_mask(lasts[here], rows, offset, chunk))
                weight_ref[head, offset - 1, here, :] = weights
                slope_ref[head, offset - 1, here, :] = slope


def attend_kernel(*refs):
    flags, (own_weight_ref, scaled_ref, sum_ref, weight_ref, own_ref, *refs) = refs[:REACH], refs[REACH:]
    taken, (att_ref, stats_ref, *blocks) = refs[: 2 * REACH], refs[2 * REACH :]
    sort_blocks(flags, taken, blocks, True)
    values = [own_ref, *blocks]
    rows, features = scaled_ref.shape
    lanes, chunks = parts_of(rows, features)
    for head, at in lanes:
        for chunk, here in chunks:
            total = dot(own_weight_ref[head, here, : here.stop], values[0][: here.stop, at], NN)
            for offset in range(REACH):
                low = here.start if offset == REACH - 1 else 0
                total += dot(weight_ref[head, offset, here, low:], values[offset + 1][low:, at], NN)
            att_ref[here, at] = total
    att = jnp.transpose(att_ref[...])
    scaled = jnp.transpose(scaled_ref[...])
    stats_ref[0:1, :] = jnp.sum(att, axis=0, keepdims=True)
    stats_ref[1:2, :] = jnp.sum(att * att, axis=0, keepdims=True)
    stats_ref[2:3, :] = sum_ref[...]
    stats_ref[3:4, :] = jnp.sum(scaled * att, axis=0, keepdims=True)


def delta_kernel(total_features, att_ref, scaled_ref, *refs):
    stats_refs, (normed_ref, delta_ref) = refs[:-2], refs[-2:]
    stats = stats_refs[0][...]
    for ref in stats_refs[1:]:
        stats += ref[...]
    width = att_ref.shape[1]
    average = stats[0:1] / total_features
    inverse = lax.rsqrt(stats[1:2] / total_features - average * average + EPSILON)
    first = stats[2:3] / total_features
    second = inverse * (stats[3:4] - average * stats[2:3]) / total_features
    average, inverse, first, second = [column(row, width) for row in (average, inverse, first, second)]
    normed = (att_ref[...] - average) * inverse
    normed_ref[...] = normed
    delta_ref[...] = (inverse * (scaled_ref[...] - first - normed * second)).astype(jnp.bfloat16)


def near_kernel(factor, q_ref, k_ref, v_ref, gate_ref, up_ref, d_ref, normed_ref, own_slope_ref,
                own_weight_t_ref, own_slope_t_ref, slope_ref, *refs):
    keys, values, refs = refs[:REACH], refs[REACH : 2 * REACH], refs[2 * REACH :]
    gq_ref, gk_ref, gv_ref, out_ref, gg_ref = refs
    rows, features = q_ref.shape
    lanes, chunks = parts_of(rows, features)
    normed = normed_ref[...]
    out_ref[...] = (normed * gate_ref[...].astype(jnp.float32)).astype(jnp.bfloat16)
    gg_ref[...] = (normed * up_ref[...].astype(jnp.float32)).astype(jnp.bfloat16)
    for head, at in lanes:
        for chunk, here in chunks:
            delta = d_ref[here, at]
            till = here.stop
            grad = dot(delta, v_ref[:till, at], NT) * own_slope_ref[head, here, :till]
            total = dot(grad.astype(jnp.bfloat16), k_ref[:till, at], NN)
            for offset in range(REACH):
                low = here.start if offset == REACH - 1 else 0
                grad = dot(delta, values[offset][low:, at], NT) * slope_ref[head, offset, here, low:]
                total += dot(grad.astype(jnp.bfloat16), keys[offset][low:, at], NN)
            gq_ref[here, at] = (total * factor).astype(jnp.bfloat16)
            low = here.start
            grad = dot(v_ref[here, at], d_ref[low:, at], NT) * own_slope_t_ref[head, here, low:]
            gk_ref[here, at] = dot(grad.astype(jnp.bfloat16), q_ref[low:, at], NN)
            gv_ref[here, at] = dot(own_weight_t_ref[head, here, low:], d_ref[low:, at], NN)


def far_kernel(factor, reach, flag_ref, v_ref, near_k_ref, near_v_ref, weight_ref, slope_ref, query_ref, first_ref,
               second_ref, gk_ref, gv_ref):
    rows, features = v_ref.shape
    lanes, chunks = parts_of(rows, features)
    last = reach == 1
    for head, at in lanes:
        for chunk, here in chunks:
            end = here.stop if reach == REACH else rows
            delta = jnp.where(flag_ref[0] == 0, first_ref[:end, at], second_ref[:end, at])
            value = near_v_ref[here, at] + dot(weight_ref[head, reach - 1, here, :end], delta, NN)
            grad = dot(v_ref[here, at], delta, NT) * slope_ref[head, reach - 1, here, :end]
            key = near_k_ref[here, at] + dot(grad.astype(jnp.bfloat16), query_ref[:end, at], NN)
            gv_ref[here, at] = value.astype(gv_ref.dtype)
            gk_ref[here, at] = (key * factor if last else key).astype(gk_ref.dtype)


def call(kernel, outs, *args, cost=None, scalars=0):
    vmem = pl.BlockSpec(memory_space=pltpu.VMEM)
    return pl.pallas_call(
        kernel,
        out_shape=[jax.ShapeDtypeStruct(shape, dtype) for shape, dtype in outs],
        in_specs=[pl.BlockSpec(memory_space=pltpu.SMEM)] * scalars + [vmem] * (len(args) - scalars),
        out_specs=[vmem] * len(outs),
        cost_estimate=cost,
        compiler_params=pltpu.CompilerParams(vmem_limit_bytes=VMEM_LIMIT),
    )(*args)


def shift(value, axis, steps, around=True):
    count = lax.axis_size(axis)
    pairs = [(source, source + steps) for source in range(count)]
    pairs = [(source, target % count) for source, target in pairs if around or 0 <= target < count]
    return lax.ppermute(value, axis, pairs)


def trade(value, steps, late):
    rows, heads = lax.axis_size("rows"), lax.axis_size("heads")
    pairs = []
    for row in range(rows):
        other = ((row - steps * late) ^ steps) + steps * late
        for head in range(heads):
            alone = row < steps * late or other >= rows
            target = (row, head ^ 1) if alone else (other, head)
            pairs.append((row * heads + head, target[0] * heads + target[1]))
    return lax.ppermute(value, ("rows", "heads"), pairs)


def copy_if(condition, pairs):
    @pl.when(condition)
    def _():
        for target, source in pairs:
            target[...] = source[...]


def pick_kernel(*refs):
    flags, (up_ref, down_ref, *refs) = refs[:REACH], refs[REACH:]
    for reach in range(REACH):
        first, second = refs[2 * reach], refs[2 * reach + 1]
        copy_if(flags[reach][0] == 0, [(first, up_ref), (second, down_ref)])
        copy_if(flags[reach][0] == 1, [(first, down_ref), (second, up_ref)])


def sort_blocks(flags, taken, blocks, before):
    for reach in range(REACH):
        first, second = taken[2 * reach], taken[2 * reach + 1]
        copy_if(flags[reach][0] == int(before), [(blocks[reach], first)])
        copy_if(flags[reach][0] == int(not before), [(blocks[reach], second)])


def meet(value, axis, step):
    count = lax.axis_size(axis)
    if count & (count - 1):
        return shift(value, axis, step)
    return lax.ppermute(value, axis, [(source, source ^ step) for source in range(count)])


def local(queries, key_vectors, value_vectors, gating, bounds, cotangent):
    block = queries.shape
    rows_dev = block[0]
    heads_dev = block[1] // DH
    factor = DH ** (-0.5)
    heads = lax.axis_size("heads")
    first_row = lax.axis_index("rows") * rows_dev
    relative = (bounds - first_row).astype(jnp.float32)
    half, full = jnp.bfloat16, jnp.float32
    square = (rows_dev, rows_dev)
    steps = range(1, REACH + 1)

    keys = [shift(key_vectors, "rows", 1), shift(key_vectors, "rows", 2)]

    order, = call(order_kernel, [((rows_dev, LANES), full)], cost=HINT)
    starts, lasts = call(column_kernel, [((rows_dev, LANES), full)] * 2, relative)
    position = lax.axis_index("rows")
    flags = [(position // reach % 2).astype(jnp.int32).reshape(1) for reach in steps]
    tied, _ = lax.optimization_barrier((value_vectors, order))
    given = call(pick_kernel, [(block, half)] * (2 * REACH), *flags, tied, queries, scalars=REACH)
    taken = [trade(given[0], 1, 0), trade(given[1], 1, 1), trade(given[2], 2, 0), trade(given[3], 2, 1)]
    own = (heads_dev, *square)
    own_weights, own_slopes, own_weights_t, own_slopes_t, scaled, scaled_sum = call(
        functools.partial(own_kernel, factor),
        [(own, half), (own, full), (own, half), (own, full), (block, full), ((1, rows_dev), full)],
        order, starts, lasts, queries, key_vectors, gating, cotangent,
    )
    pair = (heads_dev, REACH, *square)
    weights, slopes = call(
        functools.partial(weight_kernel, factor), [(pair, half), (pair, full)], starts, queries, *keys
    )
    attended, stats, *values = call(
        attend_kernel,
        [(block, full), ((4, rows_dev), full)] + [(block, half)] * REACH,
        *flags, own_weights, scaled, scaled_sum, weights, value_vectors, *taken, scalars=REACH,
    )
    weights_t, slopes_t, *later = call(
        functools.partial(later_kernel, factor),
        [(pair, half), (pair, full)] + [(block, half)] * REACH,
        *flags, lasts, key_vectors, *taken, scalars=REACH,
    )
    all_stats = [stats] + [meet(stats, "heads", step) for step in range(1, heads)]
    all_stats, weights_t = lax.optimization_barrier((all_stats, weights_t))
    normed, delta = call(
        functools.partial(delta_kernel, float(block[1] * heads)),
        [(block, full), (block, half)],
        attended, scaled, *all_stats,
    )
    delta_one = [shift(delta, "rows", -1)] * 2
    deltas = [delta_one, [trade(delta, 2, 0), trade(delta, 2, 1)]]
    grad_queries, near_key, near_value, layer_out, grad_gating = call(
        functools.partial(near_kernel, factor),
        [(block, half), (block, full), (block, full), (block, half), (block, half)],
        queries, key_vectors, value_vectors, gating, cotangent, delta, normed,
        own_slopes, own_weights_t, own_slopes_t, slopes, *keys, *values,
    )
    sums = [near_key, near_value]
    for offset in reversed(steps):
        sums = call(
            functools.partial(far_kernel, factor, offset),
            [(block, half if offset == 1 else full)] * 2,
            flags[offset - 1], value_vectors, *sums, weights_t, slopes_t, later[offset - 1], *deltas[offset - 1],
            scalars=1,
        )
    grad_keys, grad_values = sums
    return (layer_out, grad_queries, grad_keys, grad_values, grad_gating)


def solution(mesh):
    return jax.shard_map(
        local,
        mesh=mesh,
        in_specs=(
            P("rows", "heads"),
            P("rows", "heads"),
            P("rows", "heads"),
            P("rows", "heads"),
            P(None, "rows"),
            P("rows", "heads"),
        ),
        out_specs=(P("rows", "heads"),) * 5,
        check_vma=False,
    )
```

```python
import functools

import jax
import jax.numpy as jnp
from jax import lax
from jax.experimental import pallas as pl
from jax.experimental.pallas import tpu as pltpu
from jax.sharding import PartitionSpec as P

DH = 128
REACH = 2
EPSILON = 1e-05
VMEM_LIMIT = 20 * 1024 * 1024

LANES = 128
HINT = pl.CostEstimate(flops=10**10, transcendentals=0, bytes_accessed=4 * 10**7)
NT = (((1,), (1,)), ((), ()))
NN = (((1,), (0,)), ((), ()))


def dot(left, right, dims):
    return lax.dot_general(left, right, dims, preferred_element_type=jnp.float32)


def column(row, width):
    return jnp.transpose(jnp.broadcast_to(row, (width, row.shape[1])))


def lane_sums(values):
    return jnp.sum(jnp.transpose(values), axis=0, keepdims=True)


def chunk_of(rows):
    return 256 if rows % 256 == 0 else rows


def query_mask(start, rows, offset, order=None):
    keys = (lax.broadcasted_iota(jnp.int32, start.shape, 1) - offset * rows).astype(jnp.float32)
    mask = keys >= start
    if offset == 0:
        mask = mask & (keys <= order)
    return mask


def key_mask(last, rows, offset, chunk):
    size, width = last.shape
    queries = lax.broadcasted_iota(jnp.int32, (size, width), 1) + offset * rows
    mask = queries.astype(jnp.float32) <= last
    if offset == 0:
        keys = lax.broadcasted_iota(jnp.int32, (size, width), 0) + chunk * size
        mask = mask & (keys <= queries)
    return mask


def silu_and_slope(scores, mask):
    scores = jnp.where(mask, scores, 0.0)
    sigmoid = jax.nn.sigmoid(scores)
    weights = scores * sigmoid
    slope = jnp.where(mask, sigmoid + weights * (1.0 - sigmoid), 0.0)
    return weights.astype(jnp.bfloat16), slope


def parts_of(rows, features):
    size = chunk_of(rows)
    lanes = [(head, slice(head * DH, head * DH + DH)) for head in range(features // DH)]
    chunks = [(chunk, slice(chunk * size, chunk * size + size)) for chunk in range(rows // size)]
    return lanes, chunks


def widen(ref, width):
    return jnp.concatenate([ref[...]] * (width // ref.shape[1]), axis=1)


def order_kernel(order_ref):
    order_ref[...] = lax.broadcasted_iota(jnp.int32, order_ref.shape, 0).astype(jnp.float32)


def column_kernel(row_ref, start_ref, last_ref):
    start_ref[...] = column(row_ref[0:1, :], LANES)
    last_ref[...] = column(row_ref[1:2, :], LANES)


def own_kernel(factor, order_ref, start_ref, last_ref, q_ref, k_ref, gate_ref, up_ref, *refs):
    weight_ref, slope_ref, weight_t_ref, slope_t_ref, scaled_ref, sum_ref = refs
    rows, features = q_ref.shape
    lanes, chunks = parts_of(rows, features)
    starts = widen(start_ref, rows)
    lasts = widen(last_ref, rows)
    for head, at in lanes:
        for chunk, here in chunks:
            scores = dot(q_ref[here, at], k_ref[:, at], NT) * factor
            weights, slope = silu_and_slope(scores, query_mask(starts[here], rows, 0, widen(order_ref, rows)[here]))
            weight_ref[head, here, :] = weights
            slope_ref[head, here, :] = slope
            scores = dot(k_ref[here, at], q_ref[:, at], NT) * factor
            weights, slope = silu_and_slope(scores, key_mask(lasts[here], rows, 0, chunk))
            weight_t_ref[head, here, :] = weights
            slope_t_ref[head, here, :] = slope
    scaled = up_ref[...].astype(jnp.float32) * gate_ref[...].astype(jnp.float32)
    scaled_ref[...] = scaled
    sum_ref[...] = lane_sums(scaled)


def weight_kernel(factor, start_ref, q_ref, *refs):
    keys, (weight_ref, slope_ref) = refs[:REACH], refs[REACH:]
    rows, features = q_ref.shape
    lanes, chunks = parts_of(rows, features)
    starts = widen(start_ref, rows)
    for head, at in lanes:
        for chunk, here in chunks:
            for offset in range(1, REACH + 1):
                scores = dot(q_ref[here, at], keys[offset - 1][:, at], NT) * factor
                weights, slope = silu_and_slope(scores, query_mask(starts[here], rows, offset))
                weight_ref[head, offset - 1, here, :] = weights
                slope_ref[head, offset - 1, here, :] = slope


def later_kernel(factor, *refs):
    flags, (last_ref, k_ref, *refs) = refs[:REACH], refs[REACH:]
    taken, (weight_ref, slope_ref, *queries) = refs[: 2 * REACH], refs[2 * REACH :]
    sort_blocks(flags, taken, queries, False)
    rows, features = k_ref.shape
    lanes, chunks = parts_of(rows, features)
    lasts = widen(last_ref, rows)
    for head, at in lanes:
        for chunk, here in chunks:
            for offset in range(1, REACH + 1):
                scores = dot(k_ref[here, at], queries[offset - 1][:, at], NT) * factor
                weights, slope = silu_and_slope(scores, key_mask(lasts[here], rows, offset, chunk))
                weight_ref[head, offset - 1, here, :] = weights
                slope_ref[head, offset - 1, here, :] = slope


def attend_kernel(*refs):
    flags, (own_weight_ref, scaled_ref, sum_ref, weight_ref, own_ref, *refs) = refs[:REACH], refs[REACH:]
    taken, (att_ref, stats_ref, *blocks) = refs[: 2 * REACH], refs[2 * REACH :]
    sort_blocks(flags, taken, blocks, True)
    values = [own_ref, *blocks]
    rows, features = scaled_ref.shape
    lanes, chunks = parts_of(rows, features)
    for head, at in lanes:
        for chunk, here in chunks:
            total = dot(own_weight_ref[head, here, : here.stop], values[0][: here.stop, at], NN)
            for offset in range(REACH):
                low = here.start if offset == REACH - 1 else 0
                total += dot(weight_ref[head, offset, here, low:], values[offset + 1][low:, at], NN)
            att_ref[here, at] = total
    att = jnp.transpose(att_ref[...])
    scaled = jnp.transpose(scaled_ref[...])
    stats_ref[0:1, :] = jnp.sum(att, axis=0, keepdims=True)
    stats_ref[1:2, :] = jnp.sum(att * att, axis=0, keepdims=True)
    stats_ref[2:3, :] = sum_ref[...]
    stats_ref[3:4, :] = jnp.sum(scaled * att, axis=0, keepdims=True)


def delta_kernel(total_features, att_ref, scaled_ref, *refs):
    stats_refs, (normed_ref, delta_ref) = refs[:-2], refs[-2:]
    stats = stats_refs[0][...]
    for ref in stats_refs[1:]:
        stats += ref[...]
    width = att_ref.shape[1]
    average = stats[0:1] / total_features
    inverse = lax.rsqrt(stats[1:2] / total_features - average * average + EPSILON)
    first = stats[2:3] / total_features
    second = inverse * (stats[3:4] - average * stats[2:3]) / total_features
    average, inverse, first, second = [column(row, width) for row in (average, inverse, first, second)]
    normed = (att_ref[...] - average) * inverse
    normed_ref[...] = normed
    delta_ref[...] = (inverse * (scaled_ref[...] - first - normed * second)).astype(jnp.bfloat16)


def near_kernel(factor, q_ref, k_ref, v_ref, gate_ref, up_ref, d_ref, normed_ref, own_slope_ref,
                own_weight_t_ref, own_slope_t_ref, slope_ref, *refs):
    keys, values, refs = refs[:REACH], refs[REACH : 2 * REACH], refs[2 * REACH :]
    gq_ref, gk_ref, gv_ref, out_ref, gg_ref = refs
    rows, features = q_ref.shape
    lanes, chunks = parts_of(rows, features)
    normed = normed_ref[...]
    out_ref[...] = (normed * gate_ref[...].astype(jnp.float32)).astype(jnp.bfloat16)
    gg_ref[...] = (normed * up_ref[...].astype(jnp.float32)).astype(jnp.bfloat16)
    for head, at in lanes:
        for chunk, here in chunks:
            delta = d_ref[here, at]
            till = here.stop
            grad = dot(delta, v_ref[:till, at], NT) * own_slope_ref[head, here, :till]
            total = dot(grad.astype(jnp.bfloat16), k_ref[:till, at], NN)
            for offset in range(REACH):
                low = here.start if offset == REACH - 1 else 0
                grad = dot(delta, values[offset][low:, at], NT) * slope_ref[head, offset, here, low:]
                total += dot(grad.astype(jnp.bfloat16), keys[offset][low:, at], NN)
            gq_ref[here, at] = (total * factor).astype(jnp.bfloat16)
            low = here.start
            grad = dot(v_ref[here, at], d_ref[low:, at], NT) * own_slope_t_ref[head, here, low:]
            gk_ref[here, at] = dot(grad.astype(jnp.bfloat16), q_ref[low:, at], NN)
            gv_ref[here, at] = dot(own_weight_t_ref[head, here, low:], d_ref[low:, at], NN)


def far_kernel(factor, reach, flag_ref, v_ref, near_k_ref, near_v_ref, weight_ref, slope_ref, query_ref, first_ref,
               second_ref, gk_ref, gv_ref):
    rows, features = v_ref.shape
    lanes, chunks = parts_of(rows, features)
    last = reach == 1
    for head, at in lanes:
        for chunk, here in chunks:
            end = here.stop if reach == REACH else rows
            delta = jnp.where(flag_ref[0] == 0, first_ref[:end, at], second_ref[:end, at])
            value = near_v_ref[here, at] + dot(weight_ref[head, reach - 1, here, :end], delta, NN)
            grad = dot(v_ref[here, at], delta, NT) * slope_ref[head, reach - 1, here, :end]
            key = near_k_ref[here, at] + dot(grad.astype(jnp.bfloat16), query_ref[:end, at], NN)
            gv_ref[here, at] = value.astype(gv_ref.dtype)
            gk_ref[here, at] = (key * factor if last else key).astype(gk_ref.dtype)


def last_kernel(factor, v_ref, more_k_ref, more_v_ref, weight_ref, slope_ref, query_ref, d_ref, gk_ref, gv_ref,
                key_out, value_out, sems):
    rows, features = v_ref.shape
    lanes, chunks = parts_of(rows, features)
    moves = []

    def leave(source, target, here):
        move = pltpu.make_async_copy(source.at[here, :], target.at[here, :], sems.at[len(moves)])
        move.start()
        moves.append(move)

    grads = {}
    for chunk, here in chunks:
        for head, at in lanes:
            grad = dot(v_ref[here, at], d_ref[:, at], NT) * slope_ref[head, 0, here, :]
            grads[chunk, head] = grad.astype(jnp.bfloat16)
    for chunk, here in chunks:
        for head, at in lanes:
            value = more_v_ref[here, at] + dot(weight_ref[head, 0, here, :], d_ref[:, at], NN)
            value_out[here, at] = value.astype(value_out.dtype)
        leave(value_out, gv_ref, here)
    for chunk, here in chunks:
        for head, at in lanes:
            key = more_k_ref[here, at] + dot(grads[chunk, head], query_ref[:, at], NN)
            key_out[here, at] = (key * factor).astype(key_out.dtype)
        leave(key_out, gk_ref, here)
    for move in moves:
        move.wait()


def call(kernel, outs, *args, cost=None, scalars=0, place=pltpu.VMEM, scratch=()):
    vmem = pl.BlockSpec(memory_space=pltpu.VMEM)
    return pl.pallas_call(
        kernel,
        out_shape=[jax.ShapeDtypeStruct(shape, dtype) for shape, dtype in outs],
        in_specs=[pl.BlockSpec(memory_space=pltpu.SMEM)] * scalars + [vmem] * (len(args) - scalars),
        out_specs=[pl.BlockSpec(memory_space=place)] * len(outs),
        scratch_shapes=list(scratch),
        cost_estimate=cost,
        compiler_params=pltpu.CompilerParams(vmem_limit_bytes=VMEM_LIMIT),
    )(*args)


def shift(value, axis, steps, around=True):
    count = lax.axis_size(axis)
    pairs = [(source, source + steps) for source in range(count)]
    pairs = [(source, target % count) for source, target in pairs if around or 0 <= target < count]
    return lax.ppermute(value, axis, pairs)


def trade(value, steps, late):
    rows, heads = lax.axis_size("rows"), lax.axis_size("heads")
    pairs = []
    for row in range(rows):
        other = ((row - steps * late) ^ steps) + steps * late
        for head in range(heads):
            alone = row < steps * late or other >= rows
            target = (row, head ^ 1) if alone else (other, head)
            pairs.append((row * heads + head, target[0] * heads + target[1]))
    return lax.ppermute(value, ("rows", "heads"), pairs)


def copy_if(condition, pairs):
    @pl.when(condition)
    def _():
        for target, source in pairs:
            target[...] = source[...]


def pick_kernel(*refs):
    flags, (up_ref, down_ref, *refs) = refs[:REACH], refs[REACH:]
    for reach in range(REACH):
        first, second = refs[2 * reach], refs[2 * reach + 1]
        copy_if(flags[reach][0] == 0, [(first, up_ref), (second, down_ref)])
        copy_if(flags[reach][0] == 1, [(first, down_ref), (second, up_ref)])


def sort_blocks(flags, taken, blocks, before):
    for reach in range(REACH):
        first, second = taken[2 * reach], taken[2 * reach + 1]
        copy_if(flags[reach][0] == int(before), [(blocks[reach], first)])
        copy_if(flags[reach][0] == int(not before), [(blocks[reach], second)])


def meet(value, axis, step):
    count = lax.axis_size(axis)
    if count & (count - 1):
        return shift(value, axis, step)
    return lax.ppermute(value, axis, [(source, source ^ step) for source in range(count)])


def local(queries, key_vectors, value_vectors, gating, bounds, cotangent):
    block = queries.shape
    rows_dev = block[0]
    heads_dev = block[1] // DH
    factor = DH ** (-0.5)
    heads = lax.axis_size("heads")
    first_row = lax.axis_index("rows") * rows_dev
    relative = (bounds - first_row).astype(jnp.float32)
    half, full = jnp.bfloat16, jnp.float32
    square = (rows_dev, rows_dev)
    steps = range(1, REACH + 1)

    keys = [shift(key_vectors, "rows", 1), shift(key_vectors, "rows", 2)]

    order, = call(order_kernel, [((rows_dev, LANES), full)], cost=HINT)
    starts, lasts = call(column_kernel, [((rows_dev, LANES), full)] * 2, relative)
    position = lax.axis_index("rows")
    flags = [(position // reach % 2).astype(jnp.int32).reshape(1) for reach in steps]
    tied, _ = lax.optimization_barrier((value_vectors, order))
    given = call(pick_kernel, [(block, half)] * (2 * REACH), *flags, tied, queries, scalars=REACH)
    taken = [trade(given[0], 1, 0), trade(given[1], 1, 1), trade(given[2], 2, 0), trade(given[3], 2, 1)]
    own = (heads_dev, *square)
    own_weights, own_slopes, own_weights_t, own_slopes_t, scaled, scaled_sum = call(
        functools.partial(own_kernel, factor),
        [(own, half), (own, full), (own, half), (own, full), (block, full), ((1, rows_dev), full)],
        order, starts, lasts, queries, key_vectors, gating, cotangent,
    )
    pair = (heads_dev, REACH, *square)
    weights, slopes = call(
        functools.partial(weight_kernel, factor), [(pair, half), (pair, full)], starts, queries, *keys
    )
    attended, stats, *values = call(
        attend_kernel,
        [(block, full), ((4, rows_dev), full)] + [(block, half)] * REACH,
        *flags, own_weights, scaled, scaled_sum, weights, value_vectors, *taken, scalars=REACH,
    )
    weights_t, slopes_t, *later = call(
        functools.partial(later_kernel, factor),
        [(pair, half), (pair, full)] + [(block, half)] * REACH,
        *flags, lasts, key_vectors, *taken, scalars=REACH,
    )
    all_stats = [stats] + [meet(stats, "heads", step) for step in range(1, heads)]
    all_stats, weights_t = lax.optimization_barrier((all_stats, weights_t))
    normed, delta = call(
        functools.partial(delta_kernel, float(block[1] * heads)),
        [(block, full), (block, half)],
        attended, scaled, *all_stats,
    )
    delta_one = [shift(delta, "rows", -1)] * 2
    deltas = [delta_one, [trade(delta, 2, 0), trade(delta, 2, 1)]]
    grad_queries, near_key, near_value, layer_out, grad_gating = call(
        functools.partial(near_kernel, factor),
        [(block, half), (block, full), (block, full), (block, half), (block, half)],
        queries, key_vectors, value_vectors, gating, cotangent, delta, normed,
        own_slopes, own_weights_t, own_slopes_t, slopes, *keys, *values,
    )
    sums = [near_key, near_value]
    for offset in range(REACH, 1, -1):
        sums = call(
            functools.partial(far_kernel, factor, offset),
            [(block, full)] * 2,
            flags[offset - 1], value_vectors, *sums, weights_t, slopes_t, later[offset - 1], *deltas[offset - 1],
            scalars=1,
        )
    copies = 2 * (rows_dev // chunk_of(rows_dev))
    grad_keys, grad_values = call(
        functools.partial(last_kernel, factor),
        [(block, half)] * 2,
        value_vectors, *sums, weights_t, slopes_t, later[0], deltas[0][0],
        place=pl.ANY, scratch=[pltpu.VMEM(block, half)] * 2 + [pltpu.SemaphoreType.DMA((copies,))],
    )
    return (layer_out, grad_queries, grad_keys, grad_values, grad_gating)


def solution(mesh):
    return jax.shard_map(
        local,
        mesh=mesh,
        in_specs=(
            P("rows", "heads"),
            P("rows", "heads"),
            P("rows", "heads"),
            P("rows", "heads"),
            P(None, "rows"),
            P("rows", "heads"),
        ),
        out_specs=(P("rows", "heads"),) * 5,
        check_vma=False,
    )
```

```python
import functools

import jax
import jax.numpy as jnp
from jax import lax
from jax.experimental import pallas as pl
from jax.experimental.pallas import tpu as pltpu
from jax.sharding import PartitionSpec as P

DH = 128
REACH = 2
EPSILON = 1e-05
VMEM_LIMIT = 20 * 1024 * 1024

LANES = 128
HINT = pl.CostEstimate(flops=10**10, transcendentals=0, bytes_accessed=4 * 10**7)
NT = (((1,), (1,)), ((), ()))
NN = (((1,), (0,)), ((), ()))


def dot(left, right, dims):
    return lax.dot_general(left, right, dims, preferred_element_type=jnp.float32)


def column(row, width):
    return jnp.transpose(jnp.broadcast_to(row, (width, row.shape[1])))


def lane_sums(values):
    return jnp.sum(jnp.transpose(values), axis=0, keepdims=True)


def chunk_of(rows):
    return 256 if rows % 256 == 0 else rows


def query_mask(start, rows, offset, order=None):
    keys = (lax.broadcasted_iota(jnp.int32, start.shape, 1) - offset * rows).astype(jnp.float32)
    mask = keys >= start
    if offset == 0:
        mask = mask & (keys <= order)
    return mask


def key_mask(last, rows, offset, chunk):
    size, width = last.shape
    queries = lax.broadcasted_iota(jnp.int32, (size, width), 1) + offset * rows
    mask = queries.astype(jnp.float32) <= last
    if offset == 0:
        keys = lax.broadcasted_iota(jnp.int32, (size, width), 0) + chunk * size
        mask = mask & (keys <= queries)
    return mask


def silu_and_slope(scores, mask):
    scores = jnp.where(mask, scores, 0.0)
    sigmoid = jax.nn.sigmoid(scores)
    weights = scores * sigmoid
    slope = jnp.where(mask, sigmoid + weights * (1.0 - sigmoid), 0.0)
    return weights.astype(jnp.bfloat16), slope


def parts_of(rows, features):
    size = chunk_of(rows)
    lanes = [(head, slice(head * DH, head * DH + DH)) for head in range(features // DH)]
    chunks = [(chunk, slice(chunk * size, chunk * size + size)) for chunk in range(rows // size)]
    return lanes, chunks


def widen(ref, width):
    return jnp.concatenate([ref[...]] * (width // ref.shape[1]), axis=1)


def order_kernel(order_ref):
    order_ref[...] = lax.broadcasted_iota(jnp.int32, order_ref.shape, 0).astype(jnp.float32)


def column_kernel(row_ref, start_ref, last_ref):
    start_ref[...] = column(row_ref[0:1, :], LANES)
    last_ref[...] = column(row_ref[1:2, :], LANES)


def own_kernel(factor, order_ref, start_ref, last_ref, q_ref, k_ref, gate_ref, up_ref, *refs):
    weight_ref, slope_ref, weight_t_ref, slope_t_ref, scaled_ref, sum_ref = refs
    rows, features = q_ref.shape
    lanes, chunks = parts_of(rows, features)
    starts = widen(start_ref, rows)
    lasts = widen(last_ref, rows)
    for head, at in lanes:
        for chunk, here in chunks:
            scores = dot(q_ref[here, at], k_ref[:, at], NT) * factor
            weights, slope = silu_and_slope(scores, query_mask(starts[here], rows, 0, widen(order_ref, rows)[here]))
            weight_ref[head, here, :] = weights
            slope_ref[head, here, :] = slope
            scores = dot(k_ref[here, at], q_ref[:, at], NT) * factor
            weights, slope = silu_and_slope(scores, key_mask(lasts[here], rows, 0, chunk))
            weight_t_ref[head, here, :] = weights
            slope_t_ref[head, here, :] = slope
    scaled = up_ref[...].astype(jnp.float32) * gate_ref[...].astype(jnp.float32)
    scaled_ref[...] = scaled
    sum_ref[...] = lane_sums(scaled)


def weight_kernel(factor, start_ref, q_ref, *refs):
    keys, (weight_ref, slope_ref) = refs[:REACH], refs[REACH:]
    rows, features = q_ref.shape
    lanes, chunks = parts_of(rows, features)
    starts = widen(start_ref, rows)
    for head, at in lanes:
        for chunk, here in chunks:
            for offset in range(1, REACH + 1):
                scores = dot(q_ref[here, at], keys[offset - 1][:, at], NT) * factor
                weights, slope = silu_and_slope(scores, query_mask(starts[here], rows, offset))
                weight_ref[head, offset - 1, here, :] = weights
                slope_ref[head, offset - 1, here, :] = slope


def later_kernel(factor, *refs):
    flags, (last_ref, k_ref, *refs) = refs[:REACH], refs[REACH:]
    taken, (weight_ref, slope_ref, *queries) = refs[: 2 * REACH], refs[2 * REACH :]
    sort_blocks(flags, taken, queries, False)
    rows, features = k_ref.shape
    lanes, chunks = parts_of(rows, features)
    lasts = widen(last_ref, rows)
    for head, at in lanes:
        for chunk, here in chunks:
            for offset in range(1, REACH + 1):
                scores = dot(k_ref[here, at], queries[offset - 1][:, at], NT) * factor
                weights, slope = silu_and_slope(scores, key_mask(lasts[here], rows, offset, chunk))
                weight_ref[head, offset - 1, here, :] = weights
                slope_ref[head, offset - 1, here, :] = slope


def attend_kernel(*refs):
    flags, (own_weight_ref, scaled_ref, sum_ref, weight_ref, own_ref, *refs) = refs[:REACH], refs[REACH:]
    taken, (att_ref, stats_ref, *blocks) = refs[: 2 * REACH], refs[2 * REACH :]
    sort_blocks(flags, taken, blocks, True)
    values = [own_ref, *blocks]
    rows, features = scaled_ref.shape
    lanes, chunks = parts_of(rows, features)
    for head, at in lanes:
        for chunk, here in chunks:
            total = dot(own_weight_ref[head, here, : here.stop], values[0][: here.stop, at], NN)
            for offset in range(REACH):
                low = here.start if offset == REACH - 1 else 0
                total += dot(weight_ref[head, offset, here, low:], values[offset + 1][low:, at], NN)
            att_ref[here, at] = total
    att = jnp.transpose(att_ref[...])
    scaled = jnp.transpose(scaled_ref[...])
    stats_ref[0:1, :] = jnp.sum(att, axis=0, keepdims=True)
    stats_ref[1:2, :] = jnp.sum(att * att, axis=0, keepdims=True)
    stats_ref[2:3, :] = sum_ref[...]
    stats_ref[3:4, :] = jnp.sum(scaled * att, axis=0, keepdims=True)


def delta_kernel(total_features, att_ref, scaled_ref, *refs):
    stats_refs, (normed_ref, delta_ref) = refs[:-2], refs[-2:]
    stats = stats_refs[0][...]
    for ref in stats_refs[1:]:
        stats += ref[...]
    width = att_ref.shape[1]
    average = stats[0:1] / total_features
    inverse = lax.rsqrt(stats[1:2] / total_features - average * average + EPSILON)
    first = stats[2:3] / total_features
    second = inverse * (stats[3:4] - average * stats[2:3]) / total_features
    average, inverse, first, second = [column(row, width) for row in (average, inverse, first, second)]
    normed = (att_ref[...] - average) * inverse
    normed_ref[...] = normed
    delta_ref[...] = (inverse * (scaled_ref[...] - first - normed * second)).astype(jnp.bfloat16)


def near_kernel(factor, q_ref, k_ref, v_ref, gate_ref, up_ref, d_ref, normed_ref, own_slope_ref,
                own_weight_t_ref, own_slope_t_ref, slope_ref, *refs):
    keys, values, refs = refs[:REACH], refs[REACH : 2 * REACH], refs[2 * REACH :]
    gq_ref, gk_ref, gv_ref, out_ref, gg_ref = refs
    rows, features = q_ref.shape
    lanes, chunks = parts_of(rows, features)
    normed = normed_ref[...]
    out_ref[...] = (normed * gate_ref[...].astype(jnp.float32)).astype(jnp.bfloat16)
    gg_ref[...] = (normed * up_ref[...].astype(jnp.float32)).astype(jnp.bfloat16)
    for head, at in lanes:
        for chunk, here in chunks:
            delta = d_ref[here, at]
            till = here.stop
            grad = dot(delta, v_ref[:till, at], NT) * own_slope_ref[head, here, :till]
            total = dot(grad.astype(jnp.bfloat16), k_ref[:till, at], NN)
            for offset in range(REACH):
                low = here.start if offset == REACH - 1 else 0
                grad = dot(delta, values[offset][low:, at], NT) * slope_ref[head, offset, here, low:]
                total += dot(grad.astype(jnp.bfloat16), keys[offset][low:, at], NN)
            gq_ref[here, at] = (total * factor).astype(jnp.bfloat16)
            low = here.start
            grad = dot(v_ref[here, at], d_ref[low:, at], NT) * own_slope_t_ref[head, here, low:]
            gk_ref[here, at] = dot(grad.astype(jnp.bfloat16), q_ref[low:, at], NN)
            gv_ref[here, at] = dot(own_weight_t_ref[head, here, low:], d_ref[low:, at], NN)


def far_kernel(factor, reach, flag_ref, v_ref, near_k_ref, near_v_ref, weight_ref, slope_ref, query_ref, first_ref,
               second_ref, gk_ref, gv_ref):
    rows, features = v_ref.shape
    lanes, chunks = parts_of(rows, features)
    last = reach == 1
    for head, at in lanes:
        for chunk, here in chunks:
            end = here.stop if reach == REACH else rows
            delta = jnp.where(flag_ref[0] == 0, first_ref[:end, at], second_ref[:end, at])
            value = near_v_ref[here, at] + dot(weight_ref[head, reach - 1, here, :end], delta, NN)
            grad = dot(v_ref[here, at], delta, NT) * slope_ref[head, reach - 1, here, :end]
            key = near_k_ref[here, at] + dot(grad.astype(jnp.bfloat16), query_ref[:end, at], NN)
            gv_ref[here, at] = value.astype(gv_ref.dtype)
            gk_ref[here, at] = (key * factor if last else key).astype(gk_ref.dtype)


def last_kernel(factor, v_ref, more_k_ref, more_v_ref, weight_ref, slope_ref, query_ref, d_ref, gk_ref, gv_ref,
                key_out, value_out, sems):
    rows, features = v_ref.shape
    lanes, chunks = parts_of(rows, features)
    moves = []

    def leave(source, target, here):
        move = pltpu.make_async_copy(source.at[here, :], target.at[here, :], sems.at[len(moves)])
        move.start()
        moves.append(move)

    for chunk, here in chunks:
        for head, at in lanes:
            value = more_v_ref[here, at] + dot(weight_ref[head, 0, here, :], d_ref[:, at], NN)
            value_out[here, at] = value.astype(value_out.dtype)
        leave(value_out, gv_ref, here)
    grads = {}
    for chunk, here in chunks:
        for head, at in lanes:
            grad = dot(v_ref[here, at], d_ref[:, at], NT) * slope_ref[head, 0, here, :]
            grads[chunk, head] = grad.astype(jnp.bfloat16)
    for chunk, here in chunks:
        for head, at in lanes:
            key = more_k_ref[here, at] + dot(grads[chunk, head], query_ref[:, at], NN)
            key_out[here, at] = (key * factor).astype(key_out.dtype)
        leave(key_out, gk_ref, here)
    for move in moves:
        move.wait()


def call(kernel, outs, *args, cost=None, scalars=0, place=pltpu.VMEM, scratch=()):
    vmem = pl.BlockSpec(memory_space=pltpu.VMEM)
    return pl.pallas_call(
        kernel,
        out_shape=[jax.ShapeDtypeStruct(shape, dtype) for shape, dtype in outs],
        in_specs=[pl.BlockSpec(memory_space=pltpu.SMEM)] * scalars + [vmem] * (len(args) - scalars),
        out_specs=[pl.BlockSpec(memory_space=place)] * len(outs),
        scratch_shapes=list(scratch),
        cost_estimate=cost,
        compiler_params=pltpu.CompilerParams(vmem_limit_bytes=VMEM_LIMIT),
    )(*args)


def shift(value, axis, steps, around=True):
    count = lax.axis_size(axis)
    pairs = [(source, source + steps) for source in range(count)]
    pairs = [(source, target % count) for source, target in pairs if around or 0 <= target < count]
    return lax.ppermute(value, axis, pairs)


def trade(value, steps, late):
    rows, heads = lax.axis_size("rows"), lax.axis_size("heads")
    pairs = []
    for row in range(rows):
        other = ((row - steps * late) ^ steps) + steps * late
        for head in range(heads):
            alone = row < steps * late or other >= rows
            target = (row, head ^ 1) if alone else (other, head)
            pairs.append((row * heads + head, target[0] * heads + target[1]))
    return lax.ppermute(value, ("rows", "heads"), pairs)


def copy_if(condition, pairs):
    @pl.when(condition)
    def _():
        for target, source in pairs:
            target[...] = source[...]


def pick_kernel(*refs):
    flags, (up_ref, down_ref, *refs) = refs[:REACH], refs[REACH:]
    for reach in range(REACH):
        first, second = refs[2 * reach], refs[2 * reach + 1]
        copy_if(flags[reach][0] == 0, [(first, up_ref), (second, down_ref)])
        copy_if(flags[reach][0] == 1, [(first, down_ref), (second, up_ref)])


def sort_blocks(flags, taken, blocks, before):
    for reach in range(REACH):
        first, second = taken[2 * reach], taken[2 * reach + 1]
        copy_if(flags[reach][0] == int(before), [(blocks[reach], first)])
        copy_if(flags[reach][0] == int(not before), [(blocks[reach], second)])


def meet(value, axis, step):
    count = lax.axis_size(axis)
    if count & (count - 1):
        return shift(value, axis, step)
    return lax.ppermute(value, axis, [(source, source ^ step) for source in range(count)])


def local(queries, key_vectors, value_vectors, gating, bounds, cotangent):
    block = queries.shape
    rows_dev = block[0]
    heads_dev = block[1] // DH
    factor = DH ** (-0.5)
    heads = lax.axis_size("heads")
    first_row = lax.axis_index("rows") * rows_dev
    relative = (bounds - first_row).astype(jnp.float32)
    half, full = jnp.bfloat16, jnp.float32
    square = (rows_dev, rows_dev)
    steps = range(1, REACH + 1)

    keys = [shift(key_vectors, "rows", 1), shift(key_vectors, "rows", 2)]

    order, = call(order_kernel, [((rows_dev, LANES), full)], cost=HINT)
    starts, lasts = call(column_kernel, [((rows_dev, LANES), full)] * 2, relative)
    position = lax.axis_index("rows")
    flags = [(position // reach % 2).astype(jnp.int32).reshape(1) for reach in steps]
    tied, _ = lax.optimization_barrier((value_vectors, order))
    given = call(pick_kernel, [(block, half)] * (2 * REACH), *flags, tied, queries, scalars=REACH)
    taken = [trade(given[0], 1, 0), trade(given[1], 1, 1), trade(given[2], 2, 0), trade(given[3], 2, 1)]
    own = (heads_dev, *square)
    own_weights, own_slopes, own_weights_t, own_slopes_t, scaled, scaled_sum = call(
        functools.partial(own_kernel, factor),
        [(own, half), (own, full), (own, half), (own, full), (block, full), ((1, rows_dev), full)],
        order, starts, lasts, queries, key_vectors, gating, cotangent,
    )
    pair = (heads_dev, REACH, *square)
    weights, slopes = call(
        functools.partial(weight_kernel, factor), [(pair, half), (pair, full)], starts, queries, *keys
    )
    attended, stats, *values = call(
        attend_kernel,
        [(block, full), ((4, rows_dev), full)] + [(block, half)] * REACH,
        *flags, own_weights, scaled, scaled_sum, weights, value_vectors, *taken, scalars=REACH,
    )
    weights_t, slopes_t, *later = call(
        functools.partial(later_kernel, factor),
        [(pair, half), (pair, full)] + [(block, half)] * REACH,
        *flags, lasts, key_vectors, *taken, scalars=REACH,
    )
    all_stats = [stats] + [meet(stats, "heads", step) for step in range(1, heads)]
    all_stats, weights_t = lax.optimization_barrier((all_stats, weights_t))
    normed, delta = call(
        functools.partial(delta_kernel, float(block[1] * heads)),
        [(block, full), (block, half)],
        attended, scaled, *all_stats,
    )
    delta_one = [shift(delta, "rows", -1)] * 2
    deltas = [delta_one, [trade(delta, 2, 0), trade(delta, 2, 1)]]
    grad_queries, near_key, near_value, layer_out, grad_gating = call(
        functools.partial(near_kernel, factor),
        [(block, half), (block, full), (block, full), (block, half), (block, half)],
        queries, key_vectors, value_vectors, gating, cotangent, delta, normed,
        own_slopes, own_weights_t, own_slopes_t, slopes, *keys, *values,
    )
    sums = [near_key, near_value]
    for offset in range(REACH, 1, -1):
        sums = call(
            functools.partial(far_kernel, factor, offset),
            [(block, full)] * 2,
            flags[offset - 1], value_vectors, *sums, weights_t, slopes_t, later[offset - 1], *deltas[offset - 1],
            scalars=1,
        )
    copies = 2 * (rows_dev // chunk_of(rows_dev))
    grad_keys, grad_values = call(
        functools.partial(last_kernel, factor),
        [(block, half)] * 2,
        value_vectors, *sums, weights_t, slopes_t, later[0], deltas[0][0],
        place=pl.ANY, scratch=[pltpu.VMEM(block, half)] * 2 + [pltpu.SemaphoreType.DMA((copies,))],
    )
    return (layer_out, grad_queries, grad_keys, grad_values, grad_gating)


def solution(mesh):
    return jax.shard_map(
        local,
        mesh=mesh,
        in_specs=(
            P("rows", "heads"),
            P("rows", "heads"),
            P("rows", "heads"),
            P("rows", "heads"),
            P(None, "rows"),
            P("rows", "heads"),
        ),
        out_specs=(P("rows", "heads"),) * 5,
        check_vma=False,
    )
```
